256 devices in a mesh: tm: 2 (over x_hi), sx: 2 (over core), sy: 64 (over z, y, x_lo).
Axes of the slice: x: 4 (x_hi: 2, x_lo: 2; x = x_hi * 2 + x_lo), y: 4, z: 8, core: 2. Of those that a mesh axis runs over, the one named last changes fastest.
Arguments:
- u_init: float32 [128, 8192], P(None, 'sy'), may hold values from -6 to 6
- guess: float32 [16, 128, 8192], P(('tm', 'sx'), None, 'sy'), may hold values from -6 to 6
- forcing: float32 [64, 128, 8192], P(('tm', 'sx'), None, 'sy'), may hold values from -1.5 to 1.5
- speed_x: float32 [128, 8192], P(None, 'sy'), may hold values from -0.015 to 0.015
- speed_y: float32 [128, 8192], P(None, 'sy'), may hold values from -0.015 to 0.015
- diffusion: float32 [128, 8192], P(None, 'sy'), may hold values from 0.001 to 0.006
Outputs:
- solution: float32 [64, 128, 8192], P(('tm', 'sx'), None, 'sy')
The draws below stay inside these ranges and needn't reach their ends.
All inputs are finite; a program needn't handle non-finite values.
Results may differ from the reference program's by a relative error of at most 0.00002.
Values sent between devices are 32-bit elements; how exact they have to be, the bound alone decides.
A program may use at most 64 MiB of HBM per device.

```python
import math
import jax
import jax.numpy as jnp
from jax import lax

NT = 64
NX = 128
NY = 8192


def draw_forcing(key, part):
    key = jax.random.fold_in(key, 7)
    values = jnp.clip(jax.random.normal(key, (NT, NX, NY), jnp.float32), -6.0, 6.0) * 0.25
    return values


def level_of(rng, dims, shards, low, top_value):
    factor_of, own = 1.0, jax.random.fold_in(rng, 6)
    for position, blocks in shards:
        steps = jnp.exp(jax.random.uniform(jax.random.fold_in(own, position), (blocks,), jnp.float32, low / len(shards), top_value / len(shards)))
        factor_of = factor_of * jnp.repeat(steps, dims[position] // blocks).reshape([-1 if axis == position else 1 for axis in range(len(dims))])
    return factor_of


def noise(own_key, dims, deviation, reach, split=(), held_as=jnp.bfloat16):
    drawn = deviation * jax.random.normal(own_key, dims, jnp.float32)
    if split:
        drawn = drawn * level_of(own_key, dims, split, -0.22, 0.18)
    return jnp.clip(drawn, -reach, reach).astype(held_as)


def setup_inputs(seed: int = 0) -> dict:
    key_list = jax.random.split(jax.random.key(seed), 7)
    u_init = noise(key_list[0], (NX, NY), 1.0, 6.0, ((1, 64),), jnp.float32)
    guess = noise(key_list[1], (NT // 4, NX, NY), 1.0, 6.0, ((0, 4), (2, 64)), jnp.float32)
    forcing = draw_forcing(jax.random.fold_in(key_list[6], 71), 0)
    speed_x = jnp.clip(jax.random.uniform(key_list[3], (NX, NY), jnp.float32, -0.015, 0.015) * level_of(key_list[3], (NX, NY), ((1, 64),), -0.4, 0.0), -0.015, 0.015)
    speed_y = jnp.clip(jax.random.uniform(key_list[4], (NX, NY), jnp.float32, -0.015, 0.015) * level_of(key_list[4], (NX, NY), ((1, 64),), -0.4, 0.0), -0.015, 0.015)
    diffusion = jnp.clip(jnp.exp(math.log(0.006) - 1.7917594 * jax.random.uniform(key_list[5], (NX, NY), jnp.float32) ** level_of(key_list[5], (NX, NY), ((1, 64),), -0.2, 0.2)), 0.001, 0.006)
    return dict(u_init=u_init, guess=guess, forcing=forcing, speed_x=speed_x, speed_y=speed_y, diffusion=diffusion)


def slope(padded, coefficients):
    speed_x, speed_y, diffusion = coefficients
    centre = padded[..., 1:-1, 1:-1]
    west_cell = padded[..., :-2, 1:-1]
    east_cell = padded[..., 2:, 1:-1]
    south_cell = padded[..., 1:-1, :-2]
    north_cell = padded[..., 1:-1, 2:]
    along_x = jnp.maximum(speed_x, 0.0) * (centre - west_cell) + jnp.minimum(speed_x, 0.0) * (east_cell - centre)
    along_y = jnp.maximum(speed_y, 0.0) * (centre - south_cell) + jnp.minimum(speed_y, 0.0) * (north_cell - centre)
    return -along_x - along_y + diffusion * (west_cell + east_cell + south_cell + north_cell - 4.0 * centre)


def padded_field(field):
    return jnp.pad(field, ((0, 0), (1, 1), (1, 1)))


def advance(state, coefficients, factor):
    first = slope(padded_field(state), coefficients)
    middle = state + factor * first
    second = slope(padded_field(middle), coefficients)
    return state + 0.5 * factor * (first + second)


def relax_fine(starts, blocks, coefficients):
    first_f = advance(starts, coefficients, 1.0) + blocks[:, 0]
    second_f = advance(first_f, coefficients, 1.0) + blocks[:, 1]
    third_f = advance(second_f, coefficients, 1.0) + blocks[:, 2]
    return first_f, second_f, third_f


def reference(u_init, guess, forcing, speed_x, speed_y, diffusion):
    coefficients = (speed_x, speed_y, diffusion)
    blocks = forcing.reshape(NT // 4, 4, NX, NY)
    starts = jnp.concatenate([u_init[None], guess[:-1]], 0)
    first_f, second_f, third_f = relax_fine(starts, blocks, coefficients)
    resid = (blocks[:, 3] + advance(third_f, coefficients, 1.0)) - guess
    groups = resid.reshape(NT // 16, 4, NX, NY)
    lev_b = advance(groups[:, 0], coefficients, 4.0) + groups[:, 1]
    lev_c = advance(lev_b, coefficients, 4.0) + groups[:, 2]
    coarse_rhs = groups[:, 3] + advance(lev_c, coefficients, 4.0)

    def sweep(carry, term):
        following = advance(carry[None], coefficients, 16.0)[0] + term
        return following, following

    zero_state = jnp.zeros(u_init.shape, u_init.dtype)
    _, values = lax.scan(sweep, zero_state, coarse_rhs)
    before = jnp.concatenate([zero_state[None], values[:-1]], 0)
    cor_a = advance(before, coefficients, 4.0) + groups[:, 0]
    cor_b = advance(cor_a, coefficients, 4.0) + groups[:, 1]
    cor_c = advance(cor_b, coefficients, 4.0) + groups[:, 2]
    corrections = jnp.stack([cor_a, cor_b, cor_c, values], 1).reshape(NT // 4, NX, NY)
    corrected = guess + corrections
    starts_new = jnp.concatenate([u_init[None], corrected[:-1]], 0)
    fine_a, fine_b, fine_c = relax_fine(starts_new, blocks, coefficients)
    return jnp.stack([fine_a, fine_b, fine_c, corrected], 1).reshape(NT, NX, NY)
```

```python
import functools

import jax
import jax.numpy as jnp
from jax import lax
from jax.experimental import pallas as pl
from jax.experimental.pallas import tpu as pltpu
from jax.sharding import PartitionSpec as P

MESH = pl.DeviceIdType.MESH
C = 128
H = 16
W = C + 2 * H
Z = 8
N = W + 2 * Z
F32 = jnp.float32


def stencil(k, v, south, north):
    west = pltpu.roll(v, 1, 1)
    east = pltpu.roll(v, v.shape[1] - 1, 1)
    return (k[0] * v + k[1] * west) + (k[2] * east + (k[3] * south + k[4] * north))


def around(ref, at, lo, n):
    return ref[at + (pl.ds(lo, n),)], ref[at + (pl.ds(lo - 1, n),)], ref[at + (pl.ds(lo + 1, n),)]


def propagate(coef, m, src, mid, count, width, emit):
    n = C + 2 * width
    lo = Z + H - width
    k = [coef[m, j, pl.ds(H - width, n), :] for j in range(5)]
    where = [(i,) for i in range(count)] if count else [()]
    for at in where:
        v, south, north = around(src, at, lo, n)
        mid[at + (pl.ds(lo, n),)] = stencil(k, v, south, north)
    for at in where:
        v, south, north = around(mid, at, lo, n)
        emit(at, 0.5 * (src[at + (pl.ds(lo, n),)] + stencil(k, v, south, north)))


def kernel(u_hbm, guess_hbm, forcing_hbm, sx_hbm, sy_hbm, d_hbm, out,
           raw_k, raw_u, raw_g, raw_f, prev, kraw, coef, hold, g3, f2, f3, sa, sb, sc, rp, rf,
           la, lb, lc, y1p, y1, y2, y1f, y2f, e1p, e1, bf, rl, rr, yl, yr, rsl, rsr,
           lsem, ssem, rsem):
    tm, sx, c = lax.axis_index("tm"), lax.axis_index("sx"), lax.axis_index("sy")
    count = lax.axis_size("sy")
    place = 2 * tm + sx
    right, left = lax.rem(c + 1, count), lax.rem(c + count - 1, count)
    has_left = jnp.where(c > 0, 1.0, 0.0).astype(F32)
    has_right = jnp.where(c < count - 1, 1.0, 0.0).astype(F32)

    def fetch(src, dst, i):
        copy = pltpu.make_async_copy(src, dst, lsem.at[i])
        copy.start()
        return copy

    loads_k = [fetch(ref, raw_k.at[i], i) for i, ref in enumerate((sx_hbm, sy_hbm, d_hbm))]
    load_g = fetch(guess_hbm, raw_g, 3)
    load_u = fetch(u_hbm, raw_u, 4)
    load_f = fetch(forcing_hbm, raw_f, 5)

    barrier = pltpu.get_barrier_semaphore()

    def greet(*device):
        pl.semaphore_signal(barrier, inc=1, device_id=device, device_id_type=MESH)

    greet(tm, sx, left)
    greet(tm, sx, right)
    greet(tm, 1 - sx, c)

    @pl.when(place == 1)
    def _():
        greet(1, 0, c)
        greet(1, 1, c)

    @pl.when(tm == 1)
    def _():
        greet(0, 1, c)

    for ref in (sa, sb, sc, rp, rf, la, lb, lc, bf):
        ref[...] = jnp.zeros_like(ref)
    for ref in (y1p, y1f, y2f, y2, e1p, e1):
        ref[pl.ds(0, Z), :] = jnp.zeros((Z, ref.shape[1]), F32)
        ref[pl.ds(N - Z, Z), :] = jnp.zeros((Z, ref.shape[1]), F32)

    for i, load in enumerate(loads_k):
        load.wait()
        kraw[i, pl.ds(H, C), :] = raw_k[i].T

    pl.semaphore_wait(barrier, jnp.where(place == 1, 5, 3 + tm))

    sent = []

    def send(i, src, dst, device):
        copy = pltpu.make_async_remote_copy(src_ref=src, dst_ref=dst, send_sem=ssem.at[i], recv_sem=rsem.at[i],
                                            device_id=device, device_id_type=MESH)
        copy.start()
        return copy

    def both(i, to_right, at_right, to_left, at_left):
        pair = (send(i, to_right, at_right, (tm, sx, right)), send(i + 1, to_left, at_left, (tm, sx, left)))
        sent.extend(pair)
        return pair

    def arrive(*copies):
        for copy in copies:
            copy.wait_recv()

    halo_k = both(0, kraw.at[:, pl.ds(C, H), :], kraw.at[:, pl.ds(0, H), :],
                  kraw.at[:, pl.ds(H, H), :], kraw.at[:, pl.ds(H + C, H), :])

    load_g.wait()
    after = place + 1
    onward = (lax.div(after, 2), lax.rem(after, 2), c)
    prev_copy = pltpu.make_async_remote_copy(src_ref=raw_g.at[3], dst_ref=prev, send_sem=ssem.at[2], recv_sem=rsem.at[2],
                                             device_id=onward, device_id_type=MESH)

    @pl.when(place < 3)
    def _():
        prev_copy.start()

    for i in range(3):
        hold[1 + i, pl.ds(8, C), :] = raw_g[i].T
    g3[...] = raw_g[3].T
    load_u.wait()
    load_f.wait()
    for j in range(4):
        hold[4 + j, pl.ds(8, C), :] = raw_f[4 * j].T
        hold[8 + j, pl.ds(8, C), :] = raw_f[4 * j + 1].T
    halo_h = both(3, hold.at[pl.ds(1, 11), pl.ds(C, 8), :], hold.at[pl.ds(1, 11), pl.ds(0, 8), :],
                  hold.at[pl.ds(1, 11), pl.ds(8, 8), :], hold.at[pl.ds(1, 11), pl.ds(8 + C, 8), :])
    for j in range(4):
        f2[j] = raw_f[4 * j + 2].T
        f3[j] = raw_f[4 * j + 3].T

    @pl.when(place == 0)
    def _():
        hold[0, pl.ds(8, C), :] = raw_u[...].T

    @pl.when(place > 0)
    def _():
        prev_copy.wait_recv()
        hold[0, pl.ds(8, C), :] = prev[...].T

    halo_s = both(5, hold.at[0, pl.ds(C, 8), :], hold.at[0, pl.ds(0, 8), :],
                  hold.at[0, pl.ds(8, 8), :], hold.at[0, pl.ds(8 + C, 8), :])

    arrive(*halo_k)
    row = lax.broadcasted_iota(jnp.int32, (W, C), 1)
    column = lax.broadcasted_iota(jnp.int32, (W, C), 0)
    inside = jnp.where(column < H, has_left, jnp.where(column >= H + C, has_right, 1.0))
    speed_x, speed_y, diffusion = kraw[0] * inside, kraw[1] * inside, kraw[2] * inside
    west = jnp.maximum(speed_x, 0.0) + diffusion
    east = diffusion - jnp.minimum(speed_x, 0.0)
    south = jnp.maximum(speed_y, 0.0) + diffusion
    north = diffusion - jnp.minimum(speed_y, 0.0)
    centre = (west + east) + (south + north)
    west = jnp.where(row == 0, 0.0, west)
    east = jnp.where(row == C - 1, 0.0, east)
    for m, factor in enumerate((1.0, 4.0, 16.0)):
        coef[m, 0] = 1.0 - factor * centre
        coef[m, 1] = factor * west
        coef[m, 2] = factor * east
        coef[m, 3] = factor * south
        coef[m, 4] = factor * north

    main = pl.ds(Z + H, C)

    for i in range(4):
        sa[i, main, :] = hold[i, pl.ds(8, C), :]

    def into(dst, source):
        def emit(at, x):
            dst[at + (pl.ds(Z + H - 8, 8),)] = x[:8]
            dst[at + (main,)] = x[8 : 8 + C] + source(at[0])
            dst[at + (pl.ds(Z + H + C, 8),)] = x[8 + C :]
        return emit

    propagate(coef, 0, sa, sb, 4, 8, into(sc, lambda i: hold[4 + i, pl.ds(8, C), :]))
    propagate(coef, 0, sc, sb, 4, 8, into(sa, lambda i: hold[8 + i, pl.ds(8, C), :]))
    propagate(coef, 0, sa, sb, 4, 8, into(sc, lambda i: f2[i]))
    propagate(coef, 0, sc, sb, 4, 8,
              into(rp, lambda i: f3[i] - (hold[1 + i, pl.ds(8, C), :] if i < 3 else g3[...])))

    span = pl.ds(Z, W)

    def single(m, src, dst, term):
        def emit(at, x):
            dst[span, :] = x if term is None else x + term()
        propagate(coef, m, src, lb, 0, H, emit)

    single(1, rp.at[0], la, lambda: rp[1, span, :])
    single(1, la, lc, lambda: rp[2, span, :])
    single(1, lc, y2, lambda: rp[3, span, :])

    halo_r = both(7, rp.at[pl.ds(0, 3), pl.ds(Z + C, 24), :], rsl,
                  rp.at[pl.ds(0, 3), pl.ds(Z + H - 8, 24), :], rsr)

    hand = pltpu.make_async_remote_copy(src_ref=y2.at[span, :], dst_ref=y1p.at[span, :], send_sem=ssem.at[9],
                                        recv_sem=rsem.at[9], device_id=(tm, 1, c), device_id_type=MESH)

    @pl.when(sx == 0)
    def _():
        hand.start()
        y1[...] = y2[span, :]

    @pl.when(sx == 1)
    def _():
        hand.wait_recv()
        y1[...] = y1p[span, :]

    @pl.when(place == 1)
    def _():
        single(2, y1p, e1p, lambda: y2[span, :])
        yl[...] = e1p[span, :]

    @pl.when(place != 1)
    def _():
        yl[...] = y2[span, :]

    edge_1 = both(10, y1.at[pl.ds(C, 2 * H), :], rl.at[0], y1.at[pl.ds(0, 2 * H), :], rr.at[0])
    edge_2 = both(12, yl.at[pl.ds(C, 2 * H), :], rl.at[1], yl.at[pl.ds(0, 2 * H), :], rr.at[1])

    def joined(dst, own, from_left, from_right):
        dst[pl.ds(Z, 2 * H), :] = own[pl.ds(0, 2 * H), :] + has_left * from_left[...]
        dst[pl.ds(Z + 2 * H, C - 2 * H), :] = own[pl.ds(2 * H, C - 2 * H), :]
        dst[pl.ds(Z + C, 2 * H), :] = own[pl.ds(C, 2 * H), :] + has_right * from_right[...]

    arrive(*edge_2)
    joined(y2f, yl, rl.at[1], rr.at[1])

    cross = [
        pltpu.make_async_remote_copy(src_ref=y2f.at[span, :], dst_ref=e1.at[span, :], send_sem=ssem.at[14 + s],
                                     recv_sem=rsem.at[14], device_id=(1, s, c), device_id_type=MESH)
        for s in range(2)
    ]

    @pl.when(place == 1)
    def _():
        cross[1].start()
        cross[0].start()

    arrive(*edge_1)
    joined(y1f, y1, rl.at[0], rr.at[0])

    arrive(*halo_r)
    for i in range(3):
        rf[i, pl.ds(Z, 24), :] = rp[i, pl.ds(Z, 24), :] + has_left * rsl[i]
        rf[i, pl.ds(Z + 24, W - 48), :] = rp[i, pl.ds(Z + 24, W - 48), :]
        rf[i, pl.ds(Z + W - 24, 24), :] = rp[i, pl.ds(Z + W - 24, 24), :] + has_right * rsr[i]

    @pl.when(place == 0)
    def _():
        yr[...] = y1f[main, :]

    @pl.when(place == 1)
    def _():
        bf[span, :] = y1f[span, :]
        yr[...] = y2f[main, :]

    @pl.when(tm == 1)
    def _():
        cross[0].wait_recv()

    @pl.when(place == 2)
    def _():
        bf[span, :] = e1[span, :]
        single(2, bf, la, lambda: y1f[span, :])
        yr[...] = la[main, :]

    @pl.when(place == 3)
    def _():
        single(2, e1, bf, lambda: y1f[span, :])
        single(2, bf, la, lambda: y2f[span, :])
        yr[...] = la[main, :]

    arrive(*halo_h, *halo_s)

    def halo(i):
        return has_left * hold[i, pl.ds(0, 8), :], hold[i, pl.ds(8, C), :], has_right * hold[i, pl.ds(8 + C, 8), :]

    low, mid, high = pl.ds(Z + H - 8, 8), main, pl.ds(Z + H + C, 8)

    def begin(i, e):
        a, b, d = halo(i)
        sa[i, low, :] = a + e[low, :]
        if i:
            b = b + e[mid, :]
            out[4 * i - 1] = b.T
            sa[i, mid, :] = b
        else:
            sa[i, mid, :] = b + e[mid, :]
        sa[i, high, :] = d + e[high, :]

    begin(0, bf)
    single(1, bf, la, lambda: rf[0, span, :])
    begin(1, la)
    single(1, la, lc, lambda: rf[1, span, :])
    begin(2, lc)
    single(1, lc, la, lambda: rf[2, span, :])
    begin(3, la)
    out[15] = (g3[...] + yr[...]).T

    def relaxed(dst, first, step):
        def emit(at, x):
            a, b, d = halo(first + at[0])
            b = x[8 : 8 + C] + b
            out[4 * at[0] + step] = b.T
            dst[at + (low,)] = x[:8] + a
            dst[at + (mid,)] = b
            dst[at + (high,)] = x[8 + C :] + d
        return emit

    def last(at, x):
        out[4 * at[0] + 2] = (x + f2[at[0]]).T

    propagate(coef, 0, sa, sb, 4, 8, relaxed(sc, 4, 0))
    propagate(coef, 0, sc, sb, 4, 8, relaxed(sa, 8, 1))

    def final(at, x):
        last(at, x[8 : 8 + C])

    propagate(coef, 0, sa, sb, 4, 8, final)

    for copy in sent:
        copy.wait_send()

    @pl.when(place < 3)
    def _():
        prev_copy.wait_send()

    @pl.when(sx == 0)
    def _():
        hand.wait_send()

    @pl.when(place == 1)
    def _():
        cross[0].wait_send()
        cross[1].wait_send()


def local(u_init, guess, forcing, speed_x, speed_y, diffusion):
    def vmem(*shape):
        return pltpu.VMEM(shape, F32)

    any_space = pl.BlockSpec(memory_space=pltpu.HBM)
    field = (N, C)
    return pl.pallas_call(
        kernel,
        out_shape=jax.ShapeDtypeStruct(forcing.shape, F32),
        in_specs=[any_space] * 6,
        out_specs=pl.BlockSpec(memory_space=pltpu.VMEM),
        scratch_shapes=[
            vmem(3, C, C), vmem(C, C), vmem(4, C, C), vmem(16, C, C), vmem(C, C),
            vmem(3, W, C), vmem(3, 5, W, C),
            vmem(12, C + 16, C), vmem(C, C), vmem(4, C, C), vmem(4, C, C),
            vmem(4, *field), vmem(4, *field), vmem(4, *field), vmem(4, *field), vmem(3, *field),
            vmem(*field), vmem(*field), vmem(*field),
            vmem(*field), vmem(W, C), vmem(*field), vmem(*field), vmem(*field),
            vmem(*field), vmem(*field), vmem(*field),
            vmem(2, 2 * H, C), vmem(2, 2 * H, C), vmem(W, C), vmem(C, C),
            vmem(3, 24, C), vmem(3, 24, C),
            pltpu.SemaphoreType.DMA((6,)),
            pltpu.SemaphoreType.DMA((16,)),
            pltpu.SemaphoreType.DMA((16,)),
        ],
        compiler_params=pltpu.CompilerParams(collective_id=0, has_side_effects=True, vmem_limit_bytes=60 << 20),
    )(u_init, guess, forcing, speed_x, speed_y, diffusion)


def solution(mesh):
    placed = (
        P(None, "sy"),
        P(("tm", "sx"), None, "sy"),
        P(("tm", "sx"), None, "sy"),
        P(None, "sy"),
        P(None, "sy"),
        P(None, "sy"),
    )
    return jax.shard_map(
        local, mesh=mesh, in_specs=placed, out_specs=P(("tm", "sx"), None, "sy"), check_vma=False
    )
```

```python
import functools

import jax
import jax.numpy as jnp
from jax import lax
from jax.experimental import pallas as pl
from jax.experimental.pallas import tpu as pltpu
from jax.sharding import PartitionSpec as P

MESH = pl.DeviceIdType.MESH
C = 128
H = 16
W = C + 2 * H
Z = 8
N = W + 2 * Z
F32 = jnp.float32


def stencil(k, v, south, north):
    west = pltpu.roll(v, 1, 1)
    east = pltpu.roll(v, v.shape[1] - 1, 1)
    return (k[0] * v + k[1] * west) + (k[2] * east + (k[3] * south + k[4] * north))


def around(ref, at, lo, n):
    return ref[at + (pl.ds(lo, n),)], ref[at + (pl.ds(lo - 1, n),)], ref[at + (pl.ds(lo + 1, n),)]


def propagate(coef, m, src, mid, count, width, emit):
    n = C + 2 * width
    lo = Z + H - width
    k = [coef[m, j, pl.ds(H - width, n), :] for j in range(5)]
    where = [(i,) for i in range(count)] if count else [()]
    for at in where:
        v, south, north = around(src, at, lo, n)
        mid[at + (pl.ds(lo, n),)] = stencil(k, v, south, north)
    for at in where:
        v, south, north = around(mid, at, lo, n)
        emit(at, 0.5 * (src[at + (pl.ds(lo, n),)] + stencil(k, v, south, north)))


def kernel(u_hbm, guess_hbm, forcing_hbm, sx_hbm, sy_hbm, d_hbm, out,
           raw_k, raw_u, raw_g, raw_f, prev, kraw, coef, hold, g3, f2, f3, sa, sb, sc, rp, rf,
           la, lb, lc, y1p, y1, y2, y1f, y2f, e1p, e1, bf, rl, rr, yl, yr, rsl, rsr,
           lsem, ssem, rsem):
    tm, sx, c = lax.axis_index("tm"), lax.axis_index("sx"), lax.axis_index("sy")
    count = lax.axis_size("sy")
    place = 2 * tm + sx
    has_left, has_right = c > 0, c < count - 1

    def fetch(src, dst, i):
        copy = pltpu.make_async_copy(src, dst, lsem.at[i])
        copy.start()
        return copy

    loads_k = [fetch(ref, raw_k.at[i], i) for i, ref in enumerate((sx_hbm, sy_hbm, d_hbm))]
    load_g = fetch(guess_hbm, raw_g, 3)
    load_u = fetch(u_hbm, raw_u, 4)
    load_f = fetch(forcing_hbm, raw_f, 5)

    barrier = pltpu.get_barrier_semaphore()

    def greet(*device):
        pl.semaphore_signal(barrier, inc=1, device_id=device, device_id_type=MESH)

    @pl.when(has_left)
    def _():
        greet(tm, sx, c - 1)

    @pl.when(has_right)
    def _():
        greet(tm, sx, c + 1)

    greet(tm, 1 - sx, c)

    @pl.when(place == 1)
    def _():
        greet(1, 0, c)
        greet(1, 1, c)

    @pl.when(tm == 1)
    def _():
        greet(0, 1, c)

    for ref in (sa, sb, sc, rp, rf, la, lb, lc, bf):
        ref[...] = jnp.zeros_like(ref)
    for ref in (y1p, y1f, y2f, y2, e1p, e1):
        ref[pl.ds(0, Z), :] = jnp.zeros((Z, ref.shape[1]), F32)
        ref[pl.ds(N - Z, Z), :] = jnp.zeros((Z, ref.shape[1]), F32)

    @pl.when(c == 0)
    def _():
        kraw[:, pl.ds(0, H), :] = jnp.zeros((3, H, C), F32)
        hold[:, pl.ds(0, 8), :] = jnp.zeros((12, 8, C), F32)
        rl[...] = jnp.zeros_like(rl)
        rsl[...] = jnp.zeros_like(rsl)

    @pl.when(c == count - 1)
    def _():
        kraw[:, pl.ds(H + C, H), :] = jnp.zeros((3, H, C), F32)
        hold[:, pl.ds(8 + C, 8), :] = jnp.zeros((12, 8, C), F32)
        rr[...] = jnp.zeros_like(rr)
        rsr[...] = jnp.zeros_like(rsr)

    for i, load in enumerate(loads_k):
        load.wait()
        kraw[i, pl.ds(H, C), :] = raw_k[i].T

    pl.semaphore_wait(barrier, jnp.where(place == 1, 3, 1 + tm) + jnp.where(has_left, 1, 0) + jnp.where(has_right, 1, 0))

    sent = []

    def copy_of(i, src, dst, *device):
        return pltpu.make_async_remote_copy(src_ref=src, dst_ref=dst, send_sem=ssem.at[i], recv_sem=rsem.at[i],
                                            device_id=device, device_id_type=MESH)

    def both(i, to_right, at_right, to_left, at_left):
        up, down = copy_of(i, to_right, at_right, tm, sx, c + 1), copy_of(i + 1, to_left, at_left, tm, sx, c - 1)
        pl.when(has_right)(up.start)
        pl.when(has_left)(down.start)
        sent.append((up, down))
        return up, down

    def arrive(up, down):
        pl.when(has_left)(up.wait_recv)
        pl.when(has_right)(down.wait_recv)

    halo_k = both(0, kraw.at[:, pl.ds(C, H), :], kraw.at[:, pl.ds(0, H), :],
                  kraw.at[:, pl.ds(H, H), :], kraw.at[:, pl.ds(H + C, H), :])

    load_g.wait()
    after = place + 1
    onward = (lax.div(after, 2), lax.rem(after, 2), c)
    prev_copy = copy_of(2, raw_g.at[3], prev, *onward)

    @pl.when(place < 3)
    def _():
        prev_copy.start()

    for i in range(3):
        hold[1 + i, pl.ds(8, C), :] = raw_g[i].T
    g3[...] = raw_g[3].T
    load_u.wait()
    load_f.wait()
    for j in range(4):
        hold[4 + j, pl.ds(8, C), :] = raw_f[4 * j].T
        hold[8 + j, pl.ds(8, C), :] = raw_f[4 * j + 1].T
    halo_h = both(3, hold.at[pl.ds(1, 11), pl.ds(C, 8), :], hold.at[pl.ds(1, 11), pl.ds(0, 8), :],
                  hold.at[pl.ds(1, 11), pl.ds(8, 8), :], hold.at[pl.ds(1, 11), pl.ds(8 + C, 8), :])
    for j in range(4):
        f2[j] = raw_f[4 * j + 2].T
        f3[j] = raw_f[4 * j + 3].T

    @pl.when(place == 0)
    def _():
        hold[0, pl.ds(8, C), :] = raw_u[...].T

    @pl.when(place > 0)
    def _():
        prev_copy.wait_recv()
        hold[0, pl.ds(8, C), :] = prev[...].T

    halo_s = both(5, hold.at[0, pl.ds(C, 8), :], hold.at[0, pl.ds(0, 8), :],
                  hold.at[0, pl.ds(8, 8), :], hold.at[0, pl.ds(8 + C, 8), :])

    arrive(*halo_k)
    row = lax.broadcasted_iota(jnp.int32, (W, C), 1)
    speed_x, speed_y, diffusion = kraw[0], kraw[1], kraw[2]
    west = jnp.maximum(speed_x, 0.0) + diffusion
    east = diffusion - jnp.minimum(speed_x, 0.0)
    south = jnp.maximum(speed_y, 0.0) + diffusion
    north = diffusion - jnp.minimum(speed_y, 0.0)
    centre = (west + east) + (south + north)
    west = jnp.where(row == 0, 0.0, west)
    east = jnp.where(row == C - 1, 0.0, east)
    for m, factor in enumerate((1.0, 4.0, 16.0)):
        coef[m, 0] = 1.0 - factor * centre
        coef[m, 1] = factor * west
        coef[m, 2] = factor * east
        coef[m, 3] = factor * south
        coef[m, 4] = factor * north

    main = pl.ds(Z + H, C)

    for i in range(4):
        sa[i, main, :] = hold[i, pl.ds(8, C), :]

    def into(dst, source):
        def emit(at, x):
            dst[at + (pl.ds(Z + H - 8, 8),)] = x[:8]
            dst[at + (main,)] = x[8 : 8 + C] + source(at[0])
            dst[at + (pl.ds(Z + H + C, 8),)] = x[8 + C :]
        return emit

    propagate(coef, 0, sa, sb, 4, 8, into(sc, lambda i: hold[4 + i, pl.ds(8, C), :]))
    propagate(coef, 0, sc, sb, 4, 8, into(sa, lambda i: hold[8 + i, pl.ds(8, C), :]))
    propagate(coef, 0, sa, sb, 4, 8, into(sc, lambda i: f2[i]))
    propagate(coef, 0, sc, sb, 4, 8,
              into(rp, lambda i: f3[i] - (hold[1 + i, pl.ds(8, C), :] if i < 3 else g3[...])))

    span = pl.ds(Z, W)

    def single(m, src, dst, term):
        def emit(at, x):
            dst[span, :] = x if term is None else x + term()
        propagate(coef, m, src, lb, 0, H, emit)

    single(1, rp.at[0], la, lambda: rp[1, span, :])
    single(1, la, lc, lambda: rp[2, span, :])
    single(1, lc, y2, lambda: rp[3, span, :])

    halo_r = both(7, rp.at[pl.ds(0, 3), pl.ds(Z + C, 24), :], rsl,
                  rp.at[pl.ds(0, 3), pl.ds(Z + H - 8, 24), :], rsr)

    hand = copy_of(9, y2.at[span, :], y1p.at[span, :], tm, 1, c)

    @pl.when(sx == 0)
    def _():
        hand.start()
        y1[...] = y2[span, :]

    @pl.when(sx == 1)
    def _():
        hand.wait_recv()
        y1[...] = y1p[span, :]

    @pl.when(place == 1)
    def _():
        single(2, y1p, e1p, lambda: y2[span, :])
        yl[...] = e1p[span, :]

    @pl.when(place != 1)
    def _():
        yl[...] = y2[span, :]

    edge_1 = both(10, y1.at[pl.ds(C, 2 * H), :], rl.at[0], y1.at[pl.ds(0, 2 * H), :], rr.at[0])
    edge_2 = both(12, yl.at[pl.ds(C, 2 * H), :], rl.at[1], yl.at[pl.ds(0, 2 * H), :], rr.at[1])

    def joined(dst, own, from_left, from_right):
        dst[pl.ds(Z, 2 * H), :] = own[pl.ds(0, 2 * H), :] + from_left[...]
        dst[pl.ds(Z + 2 * H, C - 2 * H), :] = own[pl.ds(2 * H, C - 2 * H), :]
        dst[pl.ds(Z + C, 2 * H), :] = own[pl.ds(C, 2 * H), :] + from_right[...]

    arrive(*edge_2)
    joined(y2f, yl, rl.at[1], rr.at[1])

    cross = [
        pltpu.make_async_remote_copy(src_ref=y2f.at[span, :], dst_ref=e1.at[span, :], send_sem=ssem.at[14 + s],
                                     recv_sem=rsem.at[14], device_id=(1, s, c), device_id_type=MESH)
        for s in range(2)
    ]

    @pl.when(place == 1)
    def _():
        cross[1].start()
        cross[0].start()

    arrive(*edge_1)
    joined(y1f, y1, rl.at[0], rr.at[0])

    arrive(*halo_r)
    for i in range(3):
        rf[i, pl.ds(Z, 24), :] = rp[i, pl.ds(Z, 24), :] + rsl[i]
        rf[i, pl.ds(Z + 24, W - 48), :] = rp[i, pl.ds(Z + 24, W - 48), :]
        rf[i, pl.ds(Z + W - 24, 24), :] = rp[i, pl.ds(Z + W - 24, 24), :] + rsr[i]

    @pl.when(place == 0)
    def _():
        yr[...] = y1f[main, :]

    @pl.when(place == 1)
    def _():
        bf[span, :] = y1f[span, :]
        yr[...] = y2f[main, :]

    @pl.when(tm == 1)
    def _():
        cross[0].wait_recv()

    @pl.when(place == 2)
    def _():
        bf[span, :] = e1[span, :]
        single(2, bf, la, lambda: y1f[span, :])
        yr[...] = la[main, :]

    @pl.when(place == 3)
    def _():
        single(2, e1, bf, lambda: y1f[span, :])
        single(2, bf, la, lambda: y2f[span, :])
        yr[...] = la[main, :]

    arrive(*halo_h)
    arrive(*halo_s)

    def halo(i):
        return hold[i, pl.ds(0, 8), :], hold[i, pl.ds(8, C), :], hold[i, pl.ds(8 + C, 8), :]

    low, mid, high = pl.ds(Z + H - 8, 8), main, pl.ds(Z + H + C, 8)

    def begin(i, e):
        a, b, d = halo(i)
        sa[i, low, :] = a + e[low, :]
        if i:
            b = b + e[mid, :]
            out[4 * i - 1] = b.T
            sa[i, mid, :] = b
        else:
            sa[i, mid, :] = b + e[mid, :]
        sa[i, high, :] = d + e[high, :]

    begin(0, bf)
    single(1, bf, la, lambda: rf[0, span, :])
    begin(1, la)
    single(1, la, lc, lambda: rf[1, span, :])
    begin(2, lc)
    single(1, lc, la, lambda: rf[2, span, :])
    begin(3, la)
    out[15] = (g3[...] + yr[...]).T

    def relaxed(dst, first, step):
        def emit(at, x):
            a, b, d = halo(first + at[0])
            b = x[8 : 8 + C] + b
            out[4 * at[0] + step] = b.T
            dst[at + (low,)] = x[:8] + a
            dst[at + (mid,)] = b
            dst[at + (high,)] = x[8 + C :] + d
        return emit

    def last(at, x):
        out[4 * at[0] + 2] = (x + f2[at[0]]).T

    propagate(coef, 0, sa, sb, 4, 8, relaxed(sc, 4, 0))
    propagate(coef, 0, sc, sb, 4, 8, relaxed(sa, 8, 1))

    def final(at, x):
        last(at, x[8 : 8 + C])

    propagate(coef, 0, sa, sb, 4, 8, final)

    for up, down in sent:
        pl.when(has_right)(up.wait_send)
        pl.when(has_left)(down.wait_send)

    @pl.when(place < 3)
    def _():
        prev_copy.wait_send()

    @pl.when(sx == 0)
    def _():
        hand.wait_send()

    @pl.when(place == 1)
    def _():
        cross[0].wait_send()
        cross[1].wait_send()


def local(u_init, guess, forcing, speed_x, speed_y, diffusion):
    def vmem(*shape):
        return pltpu.VMEM(shape, F32)

    any_space = pl.BlockSpec(memory_space=pltpu.HBM)
    field = (N, C)
    return pl.pallas_call(
        kernel,
        out_shape=pltpu.VMEM(forcing.shape, F32),
        in_specs=[any_space] * 6,
        out_specs=pl.BlockSpec(memory_space=pltpu.VMEM),
        scratch_shapes=[
            vmem(3, C, C), vmem(C, C), vmem(4, C, C), vmem(16, C, C), vmem(C, C),
            vmem(3, W, C), vmem(3, 5, W, C),
            vmem(12, C + 16, C), vmem(C, C), vmem(4, C, C), vmem(4, C, C),
            vmem(4, *field), vmem(4, *field), vmem(4, *field), vmem(4, *field), vmem(3, *field),
            vmem(*field), vmem(*field), vmem(*field),
            vmem(*field), vmem(W, C), vmem(*field), vmem(*field), vmem(*field),
            vmem(*field), vmem(*field), vmem(*field),
            vmem(2, 2 * H, C), vmem(2, 2 * H, C), vmem(W, C), vmem(C, C),
            vmem(3, 24, C), vmem(3, 24, C),
            pltpu.SemaphoreType.DMA((6,)),
            pltpu.SemaphoreType.DMA((16,)),
            pltpu.SemaphoreType.DMA((16,)),
        ],
        compiler_params=pltpu.CompilerParams(collective_id=0, has_side_effects=True, vmem_limit_bytes=60 << 20),
    )(u_init, guess, forcing, speed_x, speed_y, diffusion)


def solution(mesh):
    placed = (
        P(None, "sy"),
        P(("tm", "sx"), None, "sy"),
        P(("tm", "sx"), None, "sy"),
        P(None, "sy"),
        P(None, "sy"),
        P(None, "sy"),
    )
    return jax.shard_map(
        local, mesh=mesh, in_specs=placed, out_specs=P(("tm", "sx"), None, "sy"), check_vma=False
    )
```

```python
import functools

import jax
import jax.numpy as jnp
from jax import lax
from jax.experimental import pallas as pl
from jax.experimental.pallas import tpu as pltpu
from jax.sharding import PartitionSpec as P

MESH = pl.DeviceIdType.MESH
C = 128
H = 16
W = C + 2 * H
Z = 8
N = W + 2 * Z
F32 = jnp.float32


def stencil(k, v, south, north):
    west = pltpu.roll(v, 1, 1)
    east = pltpu.roll(v, v.shape[1] - 1, 1)
    return (k[0] * v + k[1] * west) + (k[2] * east + (k[3] * south + k[4] * north))


def around(ref, at, lo, n):
    return ref[at + (pl.ds(lo, n),)], ref[at + (pl.ds(lo - 1, n),)], ref[at + (pl.ds(lo + 1, n),)]


def propagate(coef, m, src, mid, count, width, emit):
    n = C + 2 * width
    lo = Z + H - width
    k = [coef[m, j, pl.ds(H - width, n), :] for j in range(5)]
    where = [(i,) for i in range(count)] if count else [()]
    for at in where:
        v, south, north = around(src, at, lo, n)
        mid[at + (pl.ds(lo, n),)] = stencil(k, v, south, north)
    for at in where:
        v, south, north = around(mid, at, lo, n)
        emit(at, 0.5 * (src[at + (pl.ds(lo, n),)] + stencil(k, v, south, north)))


def kernel(u_hbm, guess_hbm, forcing_hbm, sx_hbm, sy_hbm, d_hbm, out,
           raw_k, raw_u, raw_g, raw_f, prev, kraw, coef, hold, g3, f2, f3, sa, sb, sc, rp, rf,
           la, lb, lc, y1p, y1, y2, y1f, y2f, e1p, e1, bf, em, el, er, rl, rr, yl, yr, rsl, rsr,
           lsem, ssem, rsem):
    tm, sx, c = lax.axis_index("tm"), lax.axis_index("sx"), lax.axis_index("sy")
    count = lax.axis_size("sy")
    place = 2 * tm + sx
    has_left, has_right = c > 0, c < count - 1
    left, right = lax.rem(c + count - 1, count), lax.rem(c + 1, count)

    def fetch(src, dst, i):
        copy = pltpu.make_async_copy(src, dst, lsem.at[i])
        copy.start()
        return copy

    loads_k = [fetch(ref, raw_k.at[i], i) for i, ref in enumerate((sx_hbm, sy_hbm, d_hbm))]
    load_g = fetch(guess_hbm, raw_g, 3)
    load_u = fetch(u_hbm, raw_u, 4)
    load_f = fetch(forcing_hbm, raw_f, 5)

    barrier = pltpu.get_barrier_semaphore()

    def greet(*device):
        pl.semaphore_signal(barrier, inc=1, device_id=device, device_id_type=MESH)

    @pl.when(has_left)
    def _():
        greet(tm, sx, c - 1)

    @pl.when(has_right)
    def _():
        greet(tm, sx, c + 1)

    greet(tm, 1 - sx, c)

    @pl.when(place == 1)
    def _():
        greet(1, 0, c)
        greet(1, 1, c)

    @pl.when(tm == 1)
    def _():
        greet(0, 1, c)

    for ref in (sa, sb, sc, rp, rf, la, lb, lc, bf):
        ref[...] = jnp.zeros_like(ref)
    for ref in (y1p, y1f, y2f, y2, e1p, e1):
        ref[pl.ds(0, Z), :] = jnp.zeros((Z, ref.shape[1]), F32)
        ref[pl.ds(N - Z, Z), :] = jnp.zeros((Z, ref.shape[1]), F32)

    @pl.when(c == 0)
    def _():
        kraw[:, pl.ds(0, H), :] = jnp.zeros((3, H, C), F32)
        hold[:, pl.ds(0, 8), :] = jnp.zeros((12, 8, C), F32)
        rl[...] = jnp.zeros_like(rl)
        rsl[...] = jnp.zeros_like(rsl)
        el[...] = jnp.zeros_like(el)

    @pl.when(c == count - 1)
    def _():
        kraw[:, pl.ds(H + C, H), :] = jnp.zeros((3, H, C), F32)
        hold[:, pl.ds(8 + C, 8), :] = jnp.zeros((12, 8, C), F32)
        rr[...] = jnp.zeros_like(rr)
        rsr[...] = jnp.zeros_like(rsr)
        er[...] = jnp.zeros_like(er)

    for i, load in enumerate(loads_k):
        load.wait()
        kraw[i, pl.ds(H, C), :] = raw_k[i].T

    pl.semaphore_wait(barrier, jnp.where(place == 1, 3, 1 + tm) + jnp.where(has_left, 1, 0) + jnp.where(has_right, 1, 0))

    sent = []

    def copy_of(i, src, dst, *device, at=None):
        return pltpu.make_async_remote_copy(src_ref=src, dst_ref=dst, send_sem=ssem.at[i], recv_sem=rsem.at[i if at is None else at],
                                            device_id=device, device_id_type=MESH)

    def both(i, to_right, at_right, to_left, at_left):
        up, down = copy_of(i, to_right, at_right, tm, sx, right), copy_of(i + 1, to_left, at_left, tm, sx, left)
        pl.when(has_right)(up.start)
        pl.when(has_left)(down.start)
        sent.append((up, down))
        return up, down

    def arrive(up, down):
        pl.when(has_left)(up.wait_recv)
        pl.when(has_right)(down.wait_recv)

    halo_k = both(0, kraw.at[:, pl.ds(C, H), :], kraw.at[:, pl.ds(0, H), :],
                  kraw.at[:, pl.ds(H, H), :], kraw.at[:, pl.ds(H + C, H), :])

    load_g.wait()
    after = place + 1
    onward = (lax.div(after, 2), lax.rem(after, 2), c)
    prev_copy = copy_of(2, raw_g.at[3], prev, *onward)

    @pl.when(place < 3)
    def _():
        prev_copy.start()

    for i in range(3):
        hold[1 + i, pl.ds(8, C), :] = raw_g[i].T
    g3[...] = raw_g[3].T
    load_u.wait()
    load_f.wait()
    for j in range(4):
        hold[4 + j, pl.ds(8, C), :] = raw_f[4 * j].T
        hold[8 + j, pl.ds(8, C), :] = raw_f[4 * j + 1].T
    halo_h = both(3, hold.at[pl.ds(1, 11), pl.ds(C, 8), :], hold.at[pl.ds(1, 11), pl.ds(0, 8), :],
                  hold.at[pl.ds(1, 11), pl.ds(8, 8), :], hold.at[pl.ds(1, 11), pl.ds(8 + C, 8), :])
    for j in range(4):
        f2[j] = raw_f[4 * j + 2].T
        f3[j] = raw_f[4 * j + 3].T

    @pl.when(place == 0)
    def _():
        hold[0, pl.ds(8, C), :] = raw_u[...].T

    @pl.when(place > 0)
    def _():
        prev_copy.wait_recv()
        hold[0, pl.ds(8, C), :] = prev[...].T

    halo_s = both(5, hold.at[0, pl.ds(C, 8), :], hold.at[0, pl.ds(0, 8), :],
                  hold.at[0, pl.ds(8, 8), :], hold.at[0, pl.ds(8 + C, 8), :])

    arrive(*halo_k)
    row = lax.broadcasted_iota(jnp.int32, (W, C), 1)
    speed_x, speed_y, diffusion = kraw[0], kraw[1], kraw[2]
    west = jnp.maximum(speed_x, 0.0) + diffusion
    east = diffusion - jnp.minimum(speed_x, 0.0)
    south = jnp.maximum(speed_y, 0.0) + diffusion
    north = diffusion - jnp.minimum(speed_y, 0.0)
    centre = (west + east) + (south + north)
    west = jnp.where(row == 0, 0.0, west)
    east = jnp.where(row == C - 1, 0.0, east)
    for m, factor in enumerate((1.0, 4.0, 16.0)):
        coef[m, 0] = 1.0 - factor * centre
        coef[m, 1] = factor * west
        coef[m, 2] = factor * east
        coef[m, 3] = factor * south
        coef[m, 4] = factor * north

    main = pl.ds(Z + H, C)

    for i in range(4):
        sa[i, main, :] = hold[i, pl.ds(8, C), :]

    def into(dst, source):
        def emit(at, x):
            dst[at + (pl.ds(Z + H - 8, 8),)] = x[:8]
            dst[at + (main,)] = x[8 : 8 + C] + source(at[0])
            dst[at + (pl.ds(Z + H + C, 8),)] = x[8 + C :]
        return emit

    propagate(coef, 0, sa, sb, 4, 8, into(sc, lambda i: hold[4 + i, pl.ds(8, C), :]))
    propagate(coef, 0, sc, sb, 4, 8, into(sa, lambda i: hold[8 + i, pl.ds(8, C), :]))
    propagate(coef, 0, sa, sb, 4, 8, into(sc, lambda i: f2[i]))
    propagate(coef, 0, sc, sb, 4, 8,
              into(rp, lambda i: f3[i] - (hold[1 + i, pl.ds(8, C), :] if i < 3 else g3[...])))

    span = pl.ds(Z, W)

    def single(m, src, dst, term):
        def emit(at, x):
            dst[span, :] = x if term is None else x + term()
        propagate(coef, m, src, lb, 0, H, emit)

    single(1, rp.at[0], la, lambda: rp[1, span, :])
    single(1, la, lc, lambda: rp[2, span, :])
    single(1, lc, y2, lambda: rp[3, span, :])

    halo_r = both(7, rp.at[pl.ds(0, 3), pl.ds(Z + C, 24), :], rsl,
                  rp.at[pl.ds(0, 3), pl.ds(Z + H - 8, 24), :], rsr)

    hand = copy_of(9, y2.at[span, :], y1p.at[span, :], tm, 1, c)

    @pl.when(sx == 0)
    def _():
        hand.start()
        y1[...] = y2[span, :]

    @pl.when(sx == 1)
    def _():
        hand.wait_recv()
        y1[...] = y1p[span, :]

    cross = []
    for s in (1, 0):
        cross.append((has_right, copy_of(16 + s, e1p.at[pl.ds(Z + C, 2 * H), :], el, 1, s, right, at=16)))
        cross.append((has_left, copy_of(18 + s, e1p.at[pl.ds(Z, 2 * H), :], er, 1, s, left, at=17)))
        cross.append((None, copy_of(14 + s, e1p.at[span, :], em, 1, s, c, at=14)))

    @pl.when(place == 1)
    def _():
        single(2, y1p, e1p, lambda: y2[span, :])
        for condition, copy in cross:
            copy.start() if condition is None else pl.when(condition)(copy.start)
        yl[...] = e1p[span, :]

    @pl.when(place != 1)
    def _():
        yl[...] = y2[span, :]

    edge_1 = both(10, y1.at[pl.ds(C, 2 * H), :], rl.at[0], y1.at[pl.ds(0, 2 * H), :], rr.at[0])
    edge_2 = both(12, yl.at[pl.ds(C, 2 * H), :], rl.at[1], yl.at[pl.ds(0, 2 * H), :], rr.at[1])

    def joined(dst, own, from_left, from_right):
        dst[pl.ds(Z, 2 * H), :] = own[pl.ds(0, 2 * H), :] + from_left[...]
        dst[pl.ds(Z + 2 * H, C - 2 * H), :] = own[pl.ds(2 * H, C - 2 * H), :]
        dst[pl.ds(Z + C, 2 * H), :] = own[pl.ds(C, 2 * H), :] + from_right[...]

    arrive(*edge_2)
    joined(y2f, yl, rl.at[1], rr.at[1])

    arrive(*edge_1)
    joined(y1f, y1, rl.at[0], rr.at[0])

    arrive(*halo_r)
    for i in range(3):
        rf[i, pl.ds(Z, 24), :] = rp[i, pl.ds(Z, 24), :] + rsl[i]
        rf[i, pl.ds(Z + 24, W - 48), :] = rp[i, pl.ds(Z + 24, W - 48), :]
        rf[i, pl.ds(Z + W - 24, 24), :] = rp[i, pl.ds(Z + W - 24, 24), :] + rsr[i]

    yr[...] = jnp.where(sx == 0, y1f[main, :], y2f[main, :])

    @pl.when(place == 1)
    def _():
        bf[span, :] = y1f[span, :]

    @pl.when(tm == 1)
    def _():
        cross[2][1].wait_recv()
        pl.when(has_left)(cross[0][1].wait_recv)
        pl.when(has_right)(cross[1][1].wait_recv)

    @pl.when(place == 2)
    def _():
        joined(bf, em, el, er)

    @pl.when(place == 3)
    def _():
        joined(e1, em, el, er)
        single(2, e1, bf, lambda: y1f[span, :])

    arrive(*halo_h)
    arrive(*halo_s)

    def halo(i):
        return hold[i, pl.ds(0, 8), :], hold[i, pl.ds(8, C), :], hold[i, pl.ds(8 + C, 8), :]

    low, mid, high = pl.ds(Z + H - 8, 8), main, pl.ds(Z + H + C, 8)

    def begin(i, e):
        a, b, d = halo(i)
        sa[i, low, :] = a + e[low, :]
        if i:
            b = b + e[mid, :]
            out[4 * i - 1] = b.T
            sa[i, mid, :] = b
        else:
            sa[i, mid, :] = b + e[mid, :]
        sa[i, high, :] = d + e[high, :]

    begin(0, bf)
    single(1, bf, la, lambda: rf[0, span, :])
    begin(1, la)
    single(1, la, lc, lambda: rf[1, span, :])
    begin(2, lc)
    single(1, lc, la, lambda: rf[2, span, :])
    begin(3, la)

    def owned(at, x):
        out[15] = (g3[...] + (yr[...] + jnp.where(place == 1, 0.0, x[8 : 8 + C]))).T


    def relaxed(dst, first, step):
        def emit(at, x):
            a, b, d = halo(first + at[0])
            b = x[8 : 8 + C] + b
            out[4 * at[0] + step] = b.T
            dst[at + (low,)] = x[:8] + a
            dst[at + (mid,)] = b
            dst[at + (high,)] = x[8 + C :] + d
        return emit

    def last(at, x):
        out[4 * at[0] + 2] = (x + f2[at[0]]).T

    propagate(coef, 0, sa, sb, 4, 8, relaxed(sc, 4, 0))
    propagate(coef, 0, sc, sb, 4, 8, relaxed(sa, 8, 1))

    def final(at, x):
        last(at, x[8 : 8 + C])

    propagate(coef, 0, sa, sb, 4, 8, final)
    propagate(coef, 2, bf, lb, 0, 8, owned)

    for up, down in sent:
        pl.when(has_right)(up.wait_send)
        pl.when(has_left)(down.wait_send)

    @pl.when(place < 3)
    def _():
        prev_copy.wait_send()

    @pl.when(sx == 0)
    def _():
        hand.wait_send()

    @pl.when(place == 1)
    def _():
        for condition, copy in cross:
            copy.wait_send() if condition is None else pl.when(condition)(copy.wait_send)


def local(u_init, guess, forcing, speed_x, speed_y, diffusion):
    def vmem(*shape):
        return pltpu.VMEM(shape, F32)

    any_space = pl.BlockSpec(memory_space=pltpu.HBM)
    field = (N, C)
    return pl.pallas_call(
        kernel,
        out_shape=pltpu.VMEM(forcing.shape, F32),
        in_specs=[any_space] * 6,
        out_specs=pl.BlockSpec(memory_space=pltpu.VMEM),
        scratch_shapes=[
            vmem(3, C, C), vmem(C, C), vmem(4, C, C), vmem(16, C, C), vmem(C, C),
            vmem(3, W, C), vmem(3, 5, W, C),
            vmem(12, C + 16, C), vmem(C, C), vmem(4, C, C), vmem(4, C, C),
            vmem(4, *field), vmem(4, *field), vmem(4, *field), vmem(4, *field), vmem(3, *field),
            vmem(*field), vmem(*field), vmem(*field),
            vmem(*field), vmem(W, C), vmem(*field), vmem(*field), vmem(*field),
            vmem(*field), vmem(*field), vmem(*field),
            vmem(W, C), vmem(2 * H, C), vmem(2 * H, C),
            vmem(2, 2 * H, C), vmem(2, 2 * H, C), vmem(W, C), vmem(C, C),
            vmem(3, 24, C), vmem(3, 24, C),
            pltpu.SemaphoreType.DMA((6,)),
            pltpu.SemaphoreType.DMA((20,)),
            pltpu.SemaphoreType.DMA((20,)),
        ],
        compiler_params=pltpu.CompilerParams(collective_id=0, has_side_effects=True, vmem_limit_bytes=60 << 20),
    )(u_init, guess, forcing, speed_x, speed_y, diffusion)


def solution(mesh):
    placed = (
        P(None, "sy"),
        P(("tm", "sx"), None, "sy"),
        P(("tm", "sx"), None, "sy"),
        P(None, "sy"),
        P(None, "sy"),
        P(None, "sy"),
    )
    return jax.shard_map(
        local, mesh=mesh, in_specs=placed, out_specs=P(("tm", "sx"), None, "sy"), check_vma=False
    )
```

```python
import functools

import jax
import jax.numpy as jnp
from jax import lax
from jax.experimental import pallas as pl
from jax.experimental.pallas import tpu as pltpu
from jax.sharding import PartitionSpec as P

MESH = pl.DeviceIdType.MESH
C = 128
H = 16
W = C + 2 * H
Z = 8
N = W + 2 * Z
F32 = jnp.float32


def west_of(x):
    return pltpu.roll(x, 1, 1)


def east_of(x):
    return pltpu.roll(x, C - 1, 1)


def build(base, coef, lo, n):
    def at(j, shift):
        return base[j, pl.ds(lo + shift, n), :]

    w, e, s, n_, c = (at(j, 0) for j in range(5))
    ww, we, ws, wn, wc = (west_of(x) for x in (w, e, s, n_, c))
    ew, ee, es, en, ec = (east_of(x) for x in (w, e, s, n_, c))
    loop = (w * we + e * ew) + (s * at(3, -1) + n_ * at(2, 1))
    centre = 0.5 * (c * c + loop)
    to_west = -0.5 * w * (c + wc)
    to_east = -0.5 * e * (c + ec)
    to_south = -0.5 * s * (c + at(4, -1))
    to_north = -0.5 * n_ * (c + at(4, 1))
    west_south = 0.5 * (w * ws + s * at(0, -1))
    west_north = 0.5 * (w * wn + n_ * at(0, 1))
    east_south = 0.5 * (e * es + s * at(1, -1))
    east_north = 0.5 * (e * en + n_ * at(1, 1))
    linear = (-c, s, n_, ew, we)
    square = (centre, to_south, to_north, east_of(to_west), west_of(to_east))
    rest = (0.5 * s * at(2, -1), 0.5 * n_ * at(3, 1), 0.5 * w * ww, 0.5 * e * ee,
            east_of(west_south), east_of(west_north), west_of(east_south), west_of(east_north))
    rows = pl.ds(lo - Z, n)
    for m, factor in enumerate((1.0, 4.0, 16.0)):
        for j in range(5):
            term = factor * linear[j] + (factor * factor) * square[j]
            coef[m, j, rows, :] = 1.0 + term if j == 0 else term
        for j in range(8):
            coef[m, 5 + j, rows, :] = (factor * factor) * rest[j]


def heun(coef, m, src, at, lo, n):
    def field(shift):
        return src[at + (pl.ds(lo + shift, n),)]

    def k(j):
        return coef[m, j, pl.ds(lo - Z, n), :]

    v, south, north = field(0), field(-1), field(1)
    from_west = k(3) * v + k(9) * south + k(10) * north
    from_east = k(4) * v + k(11) * south + k(12) * north
    columns = (k(0) * v + k(1) * south) + (k(2) * north + k(5) * field(-2)) + k(6) * field(2)
    rows = k(7) * pltpu.roll(v, 2, 1) + k(8) * pltpu.roll(v, C - 2, 1)
    return (columns + rows) + (west_of(from_west) + east_of(from_east))


def kernel(u_hbm, guess_hbm, forcing_hbm, sx_hbm, sy_hbm, d_hbm, out,
           raw_k, raw_u, raw_g, raw_f, prev, kraw, base, coef, hold, g3, f2, f3, sa, sb, sc, sd, rp, rf,
           la, lb, lc, y1p, y1, y2, y1f, y2f, e1p, e1, bf, em, el, er, rl, rr, rl2, rr2, yl, rsl, rsr, to_left, to_right, from_left, from_right,
           lsem, ssem, rsem, k_sem):
    tm, sx, c = lax.axis_index("tm"), lax.axis_index("sx"), lax.axis_index("sy")
    count = lax.axis_size("sy")
    place = 2 * tm + sx
    has_left, has_right = c > 0, c < count - 1
    left, right = lax.rem(c + count - 1, count), lax.rem(c + 1, count)

    def fetch(src, dst, i):
        copy = pltpu.make_async_copy(src, dst, lsem.at[i])
        copy.start()
        return copy

    loads_k = [fetch(ref, raw_k.at[i], i) for i, ref in enumerate((sx_hbm, sy_hbm, d_hbm))]
    load_g = fetch(guess_hbm, raw_g, 3)
    load_u = fetch(u_hbm, raw_u, 4)
    load_f = fetch(forcing_hbm, raw_f, 5)

    teller = (tm == 1) | (sx == 0)
    barrier = pltpu.get_barrier_semaphore()

    def greet(*device):
        pl.semaphore_signal(barrier, inc=1, device_id=device, device_id_type=MESH)

    @pl.when(has_left)
    def _():
        greet(tm, tm * sx, left)

    @pl.when(has_right)
    def _():
        greet(tm, tm * sx, right)

    greet(tm, 1 - sx, c)

    @pl.when(tm == 1)
    def _():
        greet(0, 0, c)
        greet(0, 1, c)

    for ref in (sa, sb, sc, sd, rp, rf, la, lb, lc, bf, base):
        ref[...] = jnp.zeros_like(ref)
    for ref in (y1p, y1f, y2, e1p, e1):
        ref[pl.ds(0, Z), :] = jnp.zeros((Z, ref.shape[1]), F32)
        ref[pl.ds(N - Z, Z), :] = jnp.zeros((Z, ref.shape[1]), F32)

    hold[:, pl.ds(0, 8), :] = jnp.zeros((12, 8, C), F32)
    hold[:, pl.ds(8 + C, 8), :] = jnp.zeros((12, 8, C), F32)

    @pl.when(c == 0)
    def _():
        kraw[:, pl.ds(0, H), :] = jnp.zeros((3, H, C), F32)
        from_left[...] = jnp.zeros_like(from_left)
        rl[...] = jnp.zeros_like(rl)
        rsl[...] = jnp.zeros_like(rsl)
        el[...] = jnp.zeros_like(el)

    @pl.when(c == count - 1)
    def _():
        kraw[:, pl.ds(H + C, H), :] = jnp.zeros((3, H, C), F32)
        from_right[...] = jnp.zeros_like(from_right)
        rr[...] = jnp.zeros_like(rr)
        rsr[...] = jnp.zeros_like(rsr)
        er[...] = jnp.zeros_like(er)

    for i, load in enumerate(loads_k):
        load.wait()
        kraw[i, pl.ds(H, C), :] = raw_k[i].T

    sides = jnp.where(has_left, 1, 0) + jnp.where(has_right, 1, 0)
    pl.semaphore_wait(barrier, 1 + jnp.where(tm == 0, 2 + 2 * (1 - sx) * sides, sides))

    sent = []

    def make_copy(src, dst, send_sem, recv_sem, *device):
        return pltpu.make_async_remote_copy(src_ref=src, dst_ref=dst, send_sem=send_sem, recv_sem=recv_sem,
                                            device_id=device, device_id_type=MESH)

    def copy_of(i, src, dst, *device, at=None):
        return make_copy(src, dst, ssem.at[i], rsem.at[i if at is None else at], *device)

    def pair(i, to_right, at_right, to_left, at_left):
        sent.append((copy_of(i, to_right, at_right, tm, sx, right), copy_of(i + 1, to_left, at_left, tm, sx, left)))
        return sent[-1]

    def tell(copies):
        pl.when(has_right)(copies[0].start)
        pl.when(has_left)(copies[1].start)

    def both(*what):
        copies = pair(*what)
        tell(copies)
        return copies

    def arrive(up, down):
        pl.when(has_left)(up.wait_recv)
        pl.when(has_right)(down.wait_recv)

    halo_k = []
    for i, to, told in ((0, tm * sx, teller), (2, 1, place == 0)):
        up = make_copy(kraw.at[:, pl.ds(C, H), :], kraw.at[:, pl.ds(0, H), :], k_sem.at[i], rsem.at[0], tm, to, right)
        down = make_copy(kraw.at[:, pl.ds(H, H), :], kraw.at[:, pl.ds(H + C, H), :], k_sem.at[i + 1], rsem.at[1],
                         tm, to, left)
        pl.when(told & has_right)(up.start)
        pl.when(told & has_left)(down.start)
        halo_k.append((up, down, told))

    load_g.wait()
    after = place + 1
    onward = (lax.div(after, 2), lax.rem(after, 2), c)
    prev_copy = copy_of(2, raw_g.at[3], prev, *onward)

    @pl.when(place < 3)
    def _():
        prev_copy.start()

    for i in range(3):
        hold[1 + i, pl.ds(8, C), :] = raw_g[i].T
    g3[...] = raw_g[3].T
    load_u.wait()
    load_f.wait()
    for j in range(4):
        hold[4 + j, pl.ds(8, C), :] = raw_f[4 * j].T
        hold[8 + j, pl.ds(8, C), :] = raw_f[4 * j + 1].T
    for i in range(4):
        to_right[i, pl.ds(6, 2), :] = hold[8 + i, pl.ds(8 + C - 2, 2), :]
        to_left[i, pl.ds(6, 2), :] = hold[8 + i, pl.ds(8, 2), :]
        to_right[4 + i // 2, pl.ds(4 * (i % 2), 4), :] = hold[4 + i, pl.ds(8 + C - 4, 4), :]
        to_left[4 + i // 2, pl.ds(4 * (i % 2), 4), :] = hold[4 + i, pl.ds(8, 4), :]
    for i in range(1, 4):
        to_right[i, pl.ds(0, 6), :] = hold[i, pl.ds(8 + C - 6, 6), :]
        to_left[i, pl.ds(0, 6), :] = hold[i, pl.ds(8, 6), :]
    tiles = pl.ds(1, 5)
    halo_h = pair(3, to_right.at[tiles], from_left.at[tiles], to_left.at[tiles], from_right.at[tiles])
    halo_s = pair(5, to_right.at[0], from_left.at[0], to_left.at[0], from_right.at[0])
    early = place != 1
    pl.when(early)(lambda: tell(halo_h))
    for j in range(4):
        f2[j] = raw_f[4 * j + 2].T
        f3[j] = raw_f[4 * j + 3].T

    @pl.when(place == 0)
    def _():
        hold[0, pl.ds(8, C), :] = raw_u[...].T

    @pl.when(place > 0)
    def _():
        prev_copy.wait_recv()
        hold[0, pl.ds(8, C), :] = prev[...].T

    to_right[0, pl.ds(0, 6), :] = hold[0, pl.ds(8 + C - 6, 6), :]
    to_left[0, pl.ds(0, 6), :] = hold[0, pl.ds(8, 6), :]
    pl.when(early)(lambda: tell(halo_s))

    def differences(lo, n):
        x, y, diffusion = (kraw[i, pl.ds(lo - Z, n), :] for i in range(3))
        row = lax.broadcasted_iota(jnp.int32, (n, C), 1)
        west = jnp.maximum(x, 0.0) + diffusion
        east = diffusion - jnp.minimum(x, 0.0)
        south = jnp.maximum(y, 0.0) + diffusion
        north = diffusion - jnp.minimum(y, 0.0)
        rows = pl.ds(lo, n)
        base[0, rows, :] = jnp.where(row == 0, 0.0, west)
        base[1, rows, :] = jnp.where(row == C - 1, 0.0, east)
        base[2, rows, :] = south
        base[3, rows, :] = north
        base[4, rows, :] = (west + east) + (south + north)

    first = Z + H
    main = pl.ds(first, C)
    span = pl.ds(Z, W)
    fields = [(i,) for i in range(4)]
    differences(first, C)
    for j in range(4):
        build(base, coef, first + 32 * j, 32)

    def source(level, i, col, n):
        if level < 2:
            return hold[4 + 4 * level + i, pl.ds(8 + col, n), :]
        if level == 2:
            return f2[i, pl.ds(col, n), :]
        at_end = hold[1 + i, pl.ds(8 + col, n), :] if i < 3 else g3[pl.ds(col, n), :]
        return f3[i, pl.ds(col, n), :] - at_end

    levels = (sa, sb, sc, sd, rp)
    for i in range(4):
        sa[i, main, :] = hold[i, pl.ds(8, C), :]
    for level in range(4):
        for col in (0, 64):
            for (i,) in fields:
                levels[level + 1][i, pl.ds(first + col, 64), :] = (
                    heun(coef, 0, levels[level], (i,), first + col, 64) + source(level, i, col, 64))

    def single(m, src, at, dst, term, parts):
        for lo, n in parts:
            dst[pl.ds(lo, n), :] = heun(coef, m, src, at, lo, n) + term(lo, n)

    def rows_of(ref, *at):
        return lambda lo, n: ref[at + (pl.ds(lo, n),)]

    def right_side(parts):
        single(1, rp, (0,), la, rows_of(rp, 1), parts)
        single(1, la, (), lb, rows_of(rp, 2), parts)
        single(1, lb, (), y2, rows_of(rp, 3), parts)

    inner = [(first + 32 * j, 32) for j in range(4)]
    whole = [(Z + 32 * j, 32) for j in range(5)]
    right_side(inner)

    arrive(*halo_k[0][:2])

    @pl.when(place == 1)
    def _():
        tell(halo_h)
        tell(halo_s)

    differences(Z, H)
    differences(first + C, H)
    build(base, coef, Z, 24)
    build(base, coef, first + C - 8, 24)
    for level in range(4):
        for (i,) in fields:
            x = heun(coef, 0, levels[level], (i,), first - 8, 16)
            levels[level + 1][i, pl.ds(first - 8, 8), :] = x[:8]
            levels[level + 1][i, pl.ds(first, 8), :] = x[8:] + source(level, i, 0, 8)
            x = heun(coef, 0, levels[level], (i,), first + C - 8, 16)
            levels[level + 1][i, pl.ds(first + C - 8, 8), :] = x[:8] + source(level, i, C - 8, 8)
            levels[level + 1][i, pl.ds(first + C, 8), :] = x[8:]

    halo_r = both(7, rp.at[0, pl.ds(Z + C, 24), :], rsl.at[0], rp.at[0, pl.ds(Z + H - 8, 24), :], rsr.at[0])
    halo_t = both(20, rp.at[pl.ds(1, 2), pl.ds(Z + C + 8, 16), :], rsl.at[pl.ds(1, 2), pl.ds(8, 16), :],
                  rp.at[pl.ds(1, 2), pl.ds(Z + H - 8, 16), :], rsr.at[pl.ds(1, 2), pl.ds(0, 16), :])

    right_side([(Z, 2 * H), (Z + C, 2 * H)])

    hand = copy_of(9, y2.at[span, :], y1p.at[span, :], tm, 1, c)

    @pl.when(sx == 0)
    def _():
        hand.start()
        y1[...] = y2[span, :]

    @pl.when(sx == 1)
    def _():
        hand.wait_recv()
        y1[...] = y1p[span, :]

    cross_main = copy_of(14, e1p.at[span, :], em, 1, 1, c)
    relay = copy_of(15, em, em, 1, 0, c, at=14)
    cross_sides = []
    for s in (1, 0):
        cross_sides.append((copy_of(16 + s, e1p.at[pl.ds(Z + C, 2 * H), :], el, 1, s, right, at=16),
                            copy_of(18 + s, e1p.at[pl.ds(Z, 2 * H), :], er, 1, s, left, at=17)))

    @pl.when(place == 1)
    def _():
        single(2, y1p, (), e1p, rows_of(y2), whole)
        cross_main.start()
        for up, down in cross_sides:
            pl.when(has_right)(up.start)
            pl.when(has_left)(down.start)
        yl[...] = e1p[span, :]

    @pl.when(place != 1)
    def _():
        yl[...] = y2[span, :]

    edge_1 = both(10, y1.at[pl.ds(C, 2 * H), :], rl, y1.at[pl.ds(0, 2 * H), :], rr)
    edge_2 = pair(12, yl.at[pl.ds(H + C, H), :], rl2, yl.at[pl.ds(0, H), :], rr2)
    pl.when(sx == 1)(lambda: tell(edge_2))

    def joined(dst, own, from_left, from_right, middle=True):
        dst[pl.ds(Z, 2 * H), :] = own[pl.ds(0, 2 * H), :] + from_left[...]
        dst[pl.ds(Z + C, 2 * H), :] = own[pl.ds(C, 2 * H), :] + from_right[...]
        if middle:
            dst[pl.ds(Z + 2 * H, C - 2 * H), :] = own[pl.ds(2 * H, C - 2 * H), :]

    y1f[pl.ds(Z + 2 * H, C - 2 * H), :] = y1[pl.ds(2 * H, C - 2 * H), :]
    y2f[pl.ds(H, C - 2 * H), :] = yl[pl.ds(2 * H, C - 2 * H), :]
    for i in range(3):
        rf[i, pl.ds(Z + 24, W - 48), :] = rp[i, pl.ds(Z + 24, W - 48), :]

    def sums():
        y2f[pl.ds(0, H), :] = yl[pl.ds(H, H), :] + rl2[...]
        y2f[pl.ds(C - H, H), :] = yl[pl.ds(C, H), :] + rr2[...]
        joined(y1f, y1, rl, rr, False)
        for i in range(3):
            if i == 0:
                rf[i, pl.ds(Z, 24), :] = rp[i, pl.ds(Z, 24), :] + rsl[i]
                rf[i, pl.ds(Z + W - 24, 24), :] = rp[i, pl.ds(Z + W - 24, 24), :] + rsr[i]
            else:
                rf[i, pl.ds(Z + 8, 16), :] = rp[i, pl.ds(Z + 8, 16), :] + rsl[i, pl.ds(8, 16), :]
                rf[i, pl.ds(Z + W - 24, 16), :] = rp[i, pl.ds(Z + W - 24, 16), :] + rsr[i, pl.ds(0, 16), :]

    later = tm == 1
    pl.when(later)(cross_main.wait_recv)
    pl.when(place == 3)(relay.start)

    @pl.when(place == 1)
    def _():
        bf[span, :] = y1p[span, :]

    @pl.when(place == 2)
    def _():
        bf[span, :] = em[...]

    @pl.when(place == 3)
    def _():
        e1[span, :] = em[...]
        single(2, e1, (), bf, rows_of(y1p), whole)

    chain = ((bf, la), (la, lb), (lb, lc))
    starts = (bf, la, lb, lc)

    for i, (src, dst) in enumerate(chain):
        single(1, src, (), dst, rows_of(rp, i), inner)
    for (i,) in fields:
        sa[i, main, :] = hold[i, pl.ds(8, C), :] + starts[i][main, :]
    for level in range(3):
        for col in (0, 64):
            for (i,) in fields:
                levels[level + 1][i, pl.ds(first + col, 64), :] = (
                    heun(coef, 0, levels[level], (i,), first + col, 64) + source(level, i, col, 64))

    for copies in (edge_1, halo_r, halo_t, halo_h, halo_s):
        arrive(*copies)
    pl.when(sx == 1)(lambda: arrive(*edge_2))

    @pl.when((sx == 0) | (c == 0))
    def _():
        rl2[...] = jnp.zeros_like(rl2)

    @pl.when((sx == 0) | (c == count - 1))
    def _():
        rr2[...] = jnp.zeros_like(rr2)

    sums()
    for i in range(4):
        hold[i, pl.ds(2, 6), :] = from_left[i, pl.ds(0, 6), :]
        hold[i, pl.ds(8 + C, 6), :] = from_right[i, pl.ds(0, 6), :]
        hold[4 + i, pl.ds(4, 4), :] = from_left[4 + i // 2, pl.ds(4 * (i % 2), 4), :]
        hold[4 + i, pl.ds(8 + C, 4), :] = from_right[4 + i // 2, pl.ds(4 * (i % 2), 4), :]
        hold[8 + i, pl.ds(6, 2), :] = from_left[i, pl.ds(6, 2), :]
        hold[8 + i, pl.ds(8 + C, 2), :] = from_right[i, pl.ds(6, 2), :]
    pl.when(later & has_left)(cross_sides[0][0].wait_recv)
    pl.when(later & has_right)(cross_sides[0][1].wait_recv)

    @pl.when(place == 1)
    def _():
        bf[span, :] = y1f[span, :]

    @pl.when(place == 2)
    def _():
        joined(bf, em, el, er)

    edges = [(Z, 48), (Z + W - 48, 48)]

    @pl.when(place == 3)
    def _():
        joined(e1, em, el, er)
        single(2, e1, (), bf, rows_of(y1f), edges)

    def correct(i):
        src, dst = chain[i]
        single(1, src, (), dst, rows_of(rf, i), edges)

    def begin(i):
        for lo in (first - 8, first + C - 32):
            sa[i, pl.ds(lo, 40), :] = hold[i, pl.ds(lo - first + 8, 40), :] + starts[i][pl.ds(lo, 40), :]
        if i:
            out[4 * i - 1] = sa[i, main, :].T

    def relax(i, level):
        for lo, n in ((first - 8, 40), (first + C - 32, 40)) if level < 2 else ((first, 32), (first + C - 32, 32)):
            levels[level + 1][i, pl.ds(lo, n), :] = (
                heun(coef, 0, levels[level], (i,), lo, n) + source(level, i, lo - first, n))
        out[4 * i + level] = levels[level + 1][i, main, :].T

    begin(0)
    correct(0)
    relax(0, 0)
    begin(1)
    correct(1)
    relax(0, 1)
    relax(1, 0)
    begin(2)
    correct(2)
    relax(0, 2)
    relax(1, 1)
    relax(2, 0)
    begin(3)
    right_after = jnp.where(sx == 0, y1f[main, :], y2f[...])
    own = jnp.concatenate([heun(coef, 2, bf, (), lo, n) for lo, n in inner], 0)
    out[15] = (g3[...] + (right_after + jnp.where(place == 1, 0.0, own))).T
    relax(1, 2)
    relax(2, 1)
    relax(3, 0)
    relax(2, 2)
    relax(3, 1)
    relax(3, 2)

    for up, down in sent:
        told = sx == 1 if up is edge_2[0] else True
        pl.when(told & has_right)(up.wait_send)
        pl.when(told & has_left)(down.wait_send)
    for up, down, told in halo_k:
        pl.when(told & has_right)(up.wait_send)
        pl.when(told & has_left)(down.wait_send)

    @pl.when(place < 3)
    def _():
        prev_copy.wait_send()

    @pl.when(sx == 0)
    def _():
        hand.wait_send()

    @pl.when(place == 1)
    def _():
        cross_main.wait_send()
        for up, down in cross_sides:
            pl.when(has_right)(up.wait_send)
            pl.when(has_left)(down.wait_send)

    pl.when(place == 3)(relay.wait_send)


def local(u_init, guess, forcing, speed_x, speed_y, diffusion):
    def vmem(*shape):
        return pltpu.VMEM(shape, F32)

    any_space = pl.BlockSpec(memory_space=pltpu.HBM)
    field = (N, C)
    return pl.pallas_call(
        kernel,
        out_shape=pltpu.VMEM(forcing.shape, F32),
        in_specs=[any_space] * 6,
        out_specs=pl.BlockSpec(memory_space=pltpu.VMEM),
        scratch_shapes=[
            vmem(3, C, C), vmem(C, C), vmem(4, C, C), vmem(16, C, C), vmem(C, C),
            vmem(3, W, C), vmem(5, *field), vmem(3, 13, W, C),
            vmem(12, C + 16, C), vmem(C, C), vmem(4, C, C), vmem(4, C, C),
            *(vmem(4, *field) for _ in range(5)), vmem(3, *field),
            vmem(*field), vmem(*field), vmem(*field),
            vmem(*field), vmem(W, C), vmem(*field), vmem(*field), vmem(C, C),
            vmem(*field), vmem(*field), vmem(*field),
            vmem(W, C), vmem(2 * H, C), vmem(2 * H, C),
            vmem(2 * H, C), vmem(2 * H, C), vmem(H, C), vmem(H, C), vmem(W, C),
            vmem(3, 24, C), vmem(3, 24, C), *(vmem(6, 8, C) for _ in range(4)),
            pltpu.SemaphoreType.DMA((6,)),
            pltpu.SemaphoreType.DMA((22,)),
            pltpu.SemaphoreType.DMA((22,)),
            pltpu.SemaphoreType.DMA((4,)),
        ],
        compiler_params=pltpu.CompilerParams(collective_id=0, has_side_effects=True, vmem_limit_bytes=60 << 20),
    )(u_init, guess, forcing, speed_x, speed_y, diffusion)


def solution(mesh):
    placed = (
        P(None, "sy"),
        P(("tm", "sx"), None, "sy"),
        P(("tm", "sx"), None, "sy"),
        P(None, "sy"),
        P(None, "sy"),
        P(None, "sy"),
    )
    return jax.shard_map(
        local, mesh=mesh, in_specs=placed, out_specs=P(("tm", "sx"), None, "sy"), check_vma=False
    )
```

```python
import functools

import jax
import jax.numpy as jnp
from jax import lax
from jax.experimental import pallas as pl
from jax.experimental.pallas import tpu as pltpu
from jax.sharding import PartitionSpec as P

MESH = pl.DeviceIdType.MESH
C = 128
H = 16
W = C + 2 * H
Z = 8
N = W + 2 * Z
F32 = jnp.float32


def west_of(x):
    return pltpu.roll(x, 1, 1)


def east_of(x):
    return pltpu.roll(x, C - 1, 1)


def build(base, coef, lo, n):
    def at(j, shift):
        return base[j, pl.ds(lo + shift, n), :]

    w, e, s, n_, c = (at(j, 0) for j in range(5))
    ww, we, ws, wn, wc = (west_of(x) for x in (w, e, s, n_, c))
    ew, ee, es, en, ec = (east_of(x) for x in (w, e, s, n_, c))
    loop = (w * we + e * ew) + (s * at(3, -1) + n_ * at(2, 1))
    centre = 0.5 * (c * c + loop)
    to_west = -0.5 * w * (c + wc)
    to_east = -0.5 * e * (c + ec)
    to_south = -0.5 * s * (c + at(4, -1))
    to_north = -0.5 * n_ * (c + at(4, 1))
    west_south = 0.5 * (w * ws + s * at(0, -1))
    west_north = 0.5 * (w * wn + n_ * at(0, 1))
    east_south = 0.5 * (e * es + s * at(1, -1))
    east_north = 0.5 * (e * en + n_ * at(1, 1))
    linear = (-c, s, n_, ew, we)
    square = (centre, to_south, to_north, east_of(to_west), west_of(to_east))
    rest = (0.5 * s * at(2, -1), 0.5 * n_ * at(3, 1), 0.5 * w * ww, 0.5 * e * ee,
            east_of(west_south), east_of(west_north), west_of(east_south), west_of(east_north))
    rows = pl.ds(lo - Z, n)
    for m, factor in enumerate((1.0, 4.0, 16.0)):
        for j in range(5):
            term = factor * linear[j] + (factor * factor) * square[j]
            coef[m, j, rows, :] = 1.0 + term if j == 0 else term
        for j in range(8):
            coef[m, 5 + j, rows, :] = (factor * factor) * rest[j]


def heun(coef, m, src, at, lo, n):
    def field(shift):
        return src[at + (pl.ds(lo + shift, n),)]

    def k(j):
        return coef[m, j, pl.ds(lo - Z, n), :]

    v, south, north = field(0), field(-1), field(1)
    from_west = k(3) * v + k(9) * south + k(10) * north
    from_east = k(4) * v + k(11) * south + k(12) * north
    columns = (k(0) * v + k(1) * south) + (k(2) * north + k(5) * field(-2)) + k(6) * field(2)
    rows = k(7) * pltpu.roll(v, 2, 1) + k(8) * pltpu.roll(v, C - 2, 1)
    return (columns + rows) + (west_of(from_west) + east_of(from_east))


def kernel(u_hbm, guess_hbm, forcing_hbm, sx_hbm, sy_hbm, d_hbm, out,
           raw_k, raw_u, raw_g, raw_f, prev, kraw, base, coef, hold, g3, f2, f3, sa, sb, sc, sd, rp, rf,
           la, lb, lc, y1p, y1, y2, y1f, y2f, e1p, e1, bf, handed, em, em_low, em_high, el, er, rl, rr, rl2, rr2, yl, rsl, rsr, to_left, to_right, from_left, from_right,
           lsem, ssem, rsem, k_sem, e_sem):
    tm, sx, c = lax.axis_index("tm"), lax.axis_index("sx"), lax.axis_index("sy")
    count = lax.axis_size("sy")
    place = 2 * tm + sx
    has_left, has_right = c > 0, c < count - 1
    left, right = lax.rem(c + count - 1, count), lax.rem(c + 1, count)

    def fetch(src, dst, i):
        copy = pltpu.make_async_copy(src, dst, lsem.at[i])
        copy.start()
        return copy

    loads_k = [fetch(ref, raw_k.at[i], i) for i, ref in enumerate((sx_hbm, sy_hbm, d_hbm))]
    load_g = fetch(guess_hbm, raw_g, 3)
    load_u = fetch(u_hbm, raw_u, 4)
    load_f = fetch(forcing_hbm, raw_f, 5)

    teller = (tm == 1) | (sx == 0)
    barrier = pltpu.get_barrier_semaphore()

    def greet(*device):
        pl.semaphore_signal(barrier, inc=1, device_id=device, device_id_type=MESH)

    @pl.when(has_left)
    def _():
        greet(tm, tm * sx, left)

    @pl.when(has_right)
    def _():
        greet(tm, tm * sx, right)

    greet(tm, 1 - sx, c)

    @pl.when(tm == 1)
    def _():
        greet(0, 0, c)
        greet(0, 1, c)

    for ref in (sa, sb, sc, sd, rp, rf, la, lb, lc, bf, base, e1p):
        ref[...] = jnp.zeros_like(ref)
    for ref in (y1p, y1f, y2, e1p, e1):
        ref[pl.ds(0, Z), :] = jnp.zeros((Z, ref.shape[1]), F32)
        ref[pl.ds(N - Z, Z), :] = jnp.zeros((Z, ref.shape[1]), F32)

    hold[:, pl.ds(0, 8), :] = jnp.zeros((12, 8, C), F32)
    hold[:, pl.ds(8 + C, 8), :] = jnp.zeros((12, 8, C), F32)

    @pl.when(c == 0)
    def _():
        kraw[:, pl.ds(0, H), :] = jnp.zeros((3, H, C), F32)
        from_left[...] = jnp.zeros_like(from_left)
        rl[...] = jnp.zeros_like(rl)
        rsl[...] = jnp.zeros_like(rsl)
        el[...] = jnp.zeros_like(el)

    @pl.when(c == count - 1)
    def _():
        kraw[:, pl.ds(H + C, H), :] = jnp.zeros((3, H, C), F32)
        from_right[...] = jnp.zeros_like(from_right)
        rr[...] = jnp.zeros_like(rr)
        rsr[...] = jnp.zeros_like(rsr)
        er[...] = jnp.zeros_like(er)

    for i, load in enumerate(loads_k):
        load.wait()
        kraw[i, pl.ds(H, C), :] = raw_k[i].T

    sides = jnp.where(has_left, 1, 0) + jnp.where(has_right, 1, 0)
    pl.semaphore_wait(barrier, 1 + jnp.where(tm == 0, 2 + 2 * (1 - sx) * sides, sides))

    sent = []

    def make_copy(src, dst, send_sem, recv_sem, *device):
        return pltpu.make_async_remote_copy(src_ref=src, dst_ref=dst, send_sem=send_sem, recv_sem=recv_sem,
                                            device_id=device, device_id_type=MESH)

    def copy_of(i, src, dst, *device, at=None):
        return make_copy(src, dst, ssem.at[i], rsem.at[i if at is None else at], *device)

    def pair(i, to_right, at_right, to_left, at_left):
        sent.append((copy_of(i, to_right, at_right, tm, sx, right), copy_of(i + 1, to_left, at_left, tm, sx, left)))
        return sent[-1]

    def tell(copies):
        pl.when(has_right)(copies[0].start)
        pl.when(has_left)(copies[1].start)

    def both(*what):
        copies = pair(*what)
        tell(copies)
        return copies

    def arrive(up, down):
        pl.when(has_left)(up.wait_recv)
        pl.when(has_right)(down.wait_recv)

    halo_k = []
    for i, to, told in ((0, tm * sx, teller), (2, 1, place == 0)):
        up = make_copy(kraw.at[:, pl.ds(C, H), :], kraw.at[:, pl.ds(0, H), :], k_sem.at[i], rsem.at[0], tm, to, right)
        down = make_copy(kraw.at[:, pl.ds(H, H), :], kraw.at[:, pl.ds(H + C, H), :], k_sem.at[i + 1], rsem.at[1],
                         tm, to, left)
        pl.when(told & has_right)(up.start)
        pl.when(told & has_left)(down.start)
        halo_k.append((up, down, told))

    load_g.wait()
    after = place + 1
    onward = (lax.div(after, 2), lax.rem(after, 2), c)
    prev_copy = copy_of(2, raw_g.at[3], prev, *onward)

    @pl.when(place < 3)
    def _():
        prev_copy.start()

    for i in range(3):
        hold[1 + i, pl.ds(8, C), :] = raw_g[i].T
    g3[...] = raw_g[3].T
    load_u.wait()
    load_f.wait()
    for j in range(4):
        hold[4 + j, pl.ds(8, C), :] = raw_f[4 * j].T
        hold[8 + j, pl.ds(8, C), :] = raw_f[4 * j + 1].T
    for i in range(4):
        to_right[i, pl.ds(6, 2), :] = hold[8 + i, pl.ds(8 + C - 2, 2), :]
        to_left[i, pl.ds(6, 2), :] = hold[8 + i, pl.ds(8, 2), :]
        to_right[4 + i // 2, pl.ds(4 * (i % 2), 4), :] = hold[4 + i, pl.ds(8 + C - 4, 4), :]
        to_left[4 + i // 2, pl.ds(4 * (i % 2), 4), :] = hold[4 + i, pl.ds(8, 4), :]
    for i in range(1, 4):
        to_right[i, pl.ds(0, 6), :] = hold[i, pl.ds(8 + C - 6, 6), :]
        to_left[i, pl.ds(0, 6), :] = hold[i, pl.ds(8, 6), :]
    tiles = pl.ds(1, 5)
    halo_h = pair(3, to_right.at[tiles], from_left.at[tiles], to_left.at[tiles], from_right.at[tiles])
    halo_s = pair(5, to_right.at[0], from_left.at[0], to_left.at[0], from_right.at[0])
    early = place != 1
    pl.when(early)(lambda: tell(halo_h))
    for j in range(4):
        f2[j] = raw_f[4 * j + 2].T
        f3[j] = raw_f[4 * j + 3].T

    def differences(lo, n):
        x, y, diffusion = (kraw[i, pl.ds(lo - Z, n), :] for i in range(3))
        row = lax.broadcasted_iota(jnp.int32, (n, C), 1)
        west = jnp.maximum(x, 0.0) + diffusion
        east = diffusion - jnp.minimum(x, 0.0)
        south = jnp.maximum(y, 0.0) + diffusion
        north = diffusion - jnp.minimum(y, 0.0)
        rows = pl.ds(lo, n)
        base[0, rows, :] = jnp.where(row == 0, 0.0, west)
        base[1, rows, :] = jnp.where(row == C - 1, 0.0, east)
        base[2, rows, :] = south
        base[3, rows, :] = north
        base[4, rows, :] = (west + east) + (south + north)

    first = Z + H
    main = pl.ds(first, C)
    span = pl.ds(Z, W)
    fields = [(i,) for i in range(4)]
    differences(first, C)
    for j in range(4):
        build(base, coef, first + 32 * j, 32)

    def source(level, i, col, n):
        if level < 2:
            return hold[4 + 4 * level + i, pl.ds(8 + col, n), :]
        if level == 2:
            return f2[i, pl.ds(col, n), :]
        at_end = hold[1 + i, pl.ds(8 + col, n), :] if i < 3 else g3[pl.ds(col, n), :]
        return f3[i, pl.ds(col, n), :] - at_end

    levels = (sa, sb, sc, sd, rp)
    def relax_inner(which):
        for i in which:
            sa[i, main, :] = hold[i, pl.ds(8, C), :]
        for level in range(4):
            for col in (0, 64):
                for i in which:
                    levels[level + 1][i, pl.ds(first + col, 64), :] = (
                        heun(coef, 0, levels[level], (i,), first + col, 64) + source(level, i, col, 64))

    relax_inner((1, 2, 3))

    @pl.when(place == 0)
    def _():
        hold[0, pl.ds(8, C), :] = raw_u[...].T

    @pl.when(place > 0)
    def _():
        prev_copy.wait_recv()
        hold[0, pl.ds(8, C), :] = prev[...].T

    to_right[0, pl.ds(0, 6), :] = hold[0, pl.ds(8 + C - 6, 6), :]
    to_left[0, pl.ds(0, 6), :] = hold[0, pl.ds(8, 6), :]
    pl.when(early)(lambda: tell(halo_s))

    relax_inner((0,))

    def single(m, src, at, dst, term, parts):
        for lo, n in parts:
            dst[pl.ds(lo, n), :] = heun(coef, m, src, at, lo, n) + term(lo, n)

    def rows_of(ref, *at):
        return lambda lo, n: ref[at + (pl.ds(lo, n),)]

    def right_side(parts):
        single(1, rp, (0,), la, rows_of(rp, 1), parts)
        single(1, la, (), lb, rows_of(rp, 2), parts)
        single(1, lb, (), y2, rows_of(rp, 3), parts)

    inner = [(first + 32 * j, 32) for j in range(4)]
    whole = [(Z + 32 * j, 32) for j in range(5)]
    right_side(inner)

    core = pl.ds(first + 16, C - 32)
    sides_of = (pl.ds(Z, 2 * H), pl.ds(Z + C, 2 * H))
    hand_in = copy_of(9, y2.at[core, :], y1p.at[core, :], tm, 1, c)
    hand_out = [copy_of(22 + i, y2.at[rows, :], handed.at[i], tm, 1, c) for i, rows in enumerate(sides_of)]
    cross_in = copy_of(14, e1p.at[core, :], em, 1, 1, c)
    relay = copy_of(15, em, em, 1, 0, c, at=14)
    low, high = pl.ds(Z, 40), pl.ds(Z + W - 40, 40)
    cross_out, cross_sides = [], []
    for s in (1, 0):
        cross_sides.append((copy_of(16 + s, e1p.at[pl.ds(Z + C, 2 * H), :], el, 1, s, right, at=16),
                            copy_of(18 + s, e1p.at[pl.ds(Z, 2 * H), :], er, 1, s, left, at=17)))
        cross_out.append((copy_of(24 + s, e1p.at[low, :], em_low, 1, s, c, at=24),
                          copy_of(26 + s, e1p.at[high, :], em_high, 1, s, c, at=25)))

    pl.when(sx == 0)(hand_in.start)
    pl.when(place == 1)(hand_in.wait_recv)

    @pl.when(place == 1)
    def _():
        single(2, y1p, (), e1p, rows_of(y2), [(first + 16, 48), (first + 64, 48)])
        cross_in.start()

    arrive(*halo_k[0][:2])

    @pl.when(place == 1)
    def _():
        tell(halo_h)
        tell(halo_s)

    differences(Z, H)
    differences(first + C, H)
    build(base, coef, Z, 24)
    build(base, coef, first + C - 8, 24)
    for level in range(4):
        for (i,) in fields:
            x = heun(coef, 0, levels[level], (i,), first - 8, 16)
            levels[level + 1][i, pl.ds(first - 8, 8), :] = x[:8]
            levels[level + 1][i, pl.ds(first, 8), :] = x[8:] + source(level, i, 0, 8)
            x = heun(coef, 0, levels[level], (i,), first + C - 8, 16)
            levels[level + 1][i, pl.ds(first + C - 8, 8), :] = x[:8] + source(level, i, C - 8, 8)
            levels[level + 1][i, pl.ds(first + C, 8), :] = x[8:]

    halo_r = both(7, rp.at[0, pl.ds(Z + C, 24), :], rsl.at[0], rp.at[0, pl.ds(Z + H - 8, 24), :], rsr.at[0])
    halo_t = both(20, rp.at[pl.ds(1, 2), pl.ds(Z + C + 8, 16), :], rsl.at[pl.ds(1, 2), pl.ds(8, 16), :],
                  rp.at[pl.ds(1, 2), pl.ds(Z + H - 8, 16), :], rsr.at[pl.ds(1, 2), pl.ds(0, 16), :])

    right_side([(Z, 2 * H), (Z + C, 2 * H)])


    edge_1 = []
    for to in range(2):
        edge_1.append((make_copy(y2.at[pl.ds(Z + C, 2 * H), :], rl, e_sem.at[2 * to], rsem.at[10], tm, to, right),
                       make_copy(y2.at[pl.ds(Z, 2 * H), :], rr, e_sem.at[2 * to + 1], rsem.at[11], tm, to, left)))

    @pl.when(sx == 0)
    def _():
        for copy in hand_out:
            copy.start()
        for to in (1, 0):
            tell(edge_1[to])
        y1[...] = y2[span, :]

    @pl.when(sx == 1)
    def _():
        pl.when(tm == 1)(hand_in.wait_recv)
        for i, copy in enumerate(hand_out):
            copy.wait_recv()
            y1p[sides_of[i], :] = handed[i]
        y1[...] = y1p[span, :]

    @pl.when(place == 1)
    def _():
        cross_in.wait_send()
        single(2, y1p, (), e1p, rows_of(y2), [(Z, 40), (Z + W - 40, 40)])
        for (up, down), outer in zip(cross_sides, cross_out):
            for copy in outer:
                copy.start()
            pl.when(has_right)(up.start)
            pl.when(has_left)(down.start)
        yl[...] = e1p[span, :]

    @pl.when(place != 1)
    def _():
        yl[...] = y2[span, :]

    edge_2 = pair(12, yl.at[pl.ds(H + C, H), :], rl2, yl.at[pl.ds(0, H), :], rr2)
    pl.when(sx == 1)(lambda: tell(edge_2))

    def joined(dst, own, from_left, from_right, middle=True):
        dst[pl.ds(Z, 2 * H), :] = own[pl.ds(0, 2 * H), :] + from_left[...]
        dst[pl.ds(Z + C, 2 * H), :] = own[pl.ds(C, 2 * H), :] + from_right[...]
        if middle:
            dst[pl.ds(Z + 2 * H, C - 2 * H), :] = own[pl.ds(2 * H, C - 2 * H), :]

    y1f[pl.ds(Z + 2 * H, C - 2 * H), :] = y1[pl.ds(2 * H, C - 2 * H), :]
    y2f[pl.ds(H, C - 2 * H), :] = yl[pl.ds(2 * H, C - 2 * H), :]
    for i in range(3):
        rf[i, pl.ds(Z + 24, W - 48), :] = rp[i, pl.ds(Z + 24, W - 48), :]

    def sums():
        joined(y1f, y1, rl, rr, False)
        for i in range(3):
            if i == 0:
                rf[i, pl.ds(Z, 24), :] = rp[i, pl.ds(Z, 24), :] + rsl[i]
                rf[i, pl.ds(Z + W - 24, 24), :] = rp[i, pl.ds(Z + W - 24, 24), :] + rsr[i]
            else:
                rf[i, pl.ds(Z + 8, 16), :] = rp[i, pl.ds(Z + 8, 16), :] + rsl[i, pl.ds(8, 16), :]
                rf[i, pl.ds(Z + W - 24, 16), :] = rp[i, pl.ds(Z + W - 24, 16), :] + rsr[i, pl.ds(0, 16), :]

    later = tm == 1
    pl.when(later)(cross_in.wait_recv)
    pl.when(place == 3)(relay.start)

    @pl.when(place == 1)
    def _():
        bf[span, :] = y1p[span, :]

    @pl.when(place == 2)
    def _():
        bf[core, :] = em[...]

    @pl.when(place == 3)
    def _():
        e1[core, :] = em[...]
        single(2, e1, (), bf, rows_of(y1p), inner)

    chain = ((bf, la), (la, lb), (lb, lc))
    starts = (bf, la, lb, lc)

    for i, (src, dst) in enumerate(chain):
        single(1, src, (), dst, rows_of(rp, i), inner)
    for (i,) in fields:
        sa[i, main, :] = hold[i, pl.ds(8, C), :] + starts[i][main, :]
    for level in range(3):
        for col in (0, 64):
            for (i,) in fields:
                levels[level + 1][i, pl.ds(first + col, 64), :] = (
                    heun(coef, 0, levels[level], (i,), first + col, 64) + source(level, i, col, 64))

    for copies in (edge_1[0], halo_r, halo_t, halo_h, halo_s):
        arrive(*copies)
    sums()
    for i in range(4):
        hold[i, pl.ds(2, 6), :] = from_left[i, pl.ds(0, 6), :]
        hold[i, pl.ds(8 + C, 6), :] = from_right[i, pl.ds(0, 6), :]
        hold[4 + i, pl.ds(4, 4), :] = from_left[4 + i // 2, pl.ds(4 * (i % 2), 4), :]
        hold[4 + i, pl.ds(8 + C, 4), :] = from_right[4 + i // 2, pl.ds(4 * (i % 2), 4), :]
        hold[8 + i, pl.ds(6, 2), :] = from_left[i, pl.ds(6, 2), :]
        hold[8 + i, pl.ds(8 + C, 2), :] = from_right[i, pl.ds(6, 2), :]
    @pl.when(later)
    def _():
        for copy in cross_out[0]:
            copy.wait_recv()

    pl.when(later & has_left)(cross_sides[0][0].wait_recv)
    pl.when(later & has_right)(cross_sides[0][1].wait_recv)

    edges = [(Z, 48), (Z + W - 48, 48)]

    def crossed(dst):
        dst[pl.ds(Z, 2 * H), :] = em_low[pl.ds(0, 2 * H), :] + el[...]
        dst[pl.ds(Z + 2 * H, 8), :] = em_low[pl.ds(2 * H, 8), :]
        dst[pl.ds(Z + C - 8, 8), :] = em_high[pl.ds(0, 8), :]
        dst[pl.ds(Z + C, 2 * H), :] = em_high[pl.ds(8, 2 * H), :] + er[...]

    @pl.when(place == 1)
    def _():
        bf[span, :] = y1f[span, :]

    @pl.when(place == 2)
    def _():
        crossed(bf)


    @pl.when(place == 3)
    def _():
        crossed(e1)
        single(2, e1, (), bf, rows_of(y1f), edges)

    def correct(i):
        src, dst = chain[i]
        single(1, src, (), dst, rows_of(rf, i), edges)

    def begin(i):
        for lo in (first - 8, first + C - 32):
            sa[i, pl.ds(lo, 40), :] = hold[i, pl.ds(lo - first + 8, 40), :] + starts[i][pl.ds(lo, 40), :]
        if i:
            out[4 * i - 1] = sa[i, main, :].T

    def relax(i, level):
        for lo, n in ((first - 8, 40), (first + C - 32, 40)) if level < 2 else ((first, 32), (first + C - 32, 32)):
            levels[level + 1][i, pl.ds(lo, n), :] = (
                heun(coef, 0, levels[level], (i,), lo, n) + source(level, i, lo - first, n))
        out[4 * i + level] = levels[level + 1][i, main, :].T

    begin(0)
    correct(0)
    relax(0, 0)
    begin(1)
    correct(1)
    relax(0, 1)
    relax(1, 0)
    begin(2)
    correct(2)
    relax(0, 2)
    relax(1, 1)
    relax(2, 0)
    begin(3)
    relax(1, 2)
    relax(2, 1)
    relax(3, 0)
    relax(2, 2)
    relax(3, 1)
    relax(3, 2)
    pl.when(sx == 1)(lambda: arrive(*edge_2))

    @pl.when((sx == 0) | (c == 0))
    def _():
        rl2[...] = jnp.zeros_like(rl2)

    @pl.when((sx == 0) | (c == count - 1))
    def _():
        rr2[...] = jnp.zeros_like(rr2)

    y2f[pl.ds(0, H), :] = yl[pl.ds(H, H), :] + rl2[...]
    y2f[pl.ds(C - H, H), :] = yl[pl.ds(C, H), :] + rr2[...]
    right_after = jnp.where(sx == 0, y1f[main, :], y2f[...])
    own = jnp.concatenate([heun(coef, 2, bf, (), lo, n) for lo, n in inner], 0)
    out[15] = (g3[...] + (right_after + jnp.where(place == 1, 0.0, own))).T

    for up, down in sent:
        told = sx == 1 if up is edge_2[0] else True
        pl.when(told & has_right)(up.wait_send)
        pl.when(told & has_left)(down.wait_send)
    for up, down, told in halo_k + [copies + (sx == 0,) for copies in edge_1]:
        pl.when(told & has_right)(up.wait_send)
        pl.when(told & has_left)(down.wait_send)

    @pl.when(place < 3)
    def _():
        prev_copy.wait_send()

    @pl.when(sx == 0)
    def _():
        hand_in.wait_send()
        for copy in hand_out:
            copy.wait_send()

    @pl.when(place == 1)
    def _():
        for copy in cross_out[0] + cross_out[1]:
            copy.wait_send()
        for up, down in cross_sides:
            pl.when(has_right)(up.wait_send)
            pl.when(has_left)(down.wait_send)

    pl.when(place == 3)(relay.wait_send)


def local(u_init, guess, forcing, speed_x, speed_y, diffusion):
    def vmem(*shape):
        return pltpu.VMEM(shape, F32)

    any_space = pl.BlockSpec(memory_space=pltpu.HBM)
    field = (N, C)
    return pl.pallas_call(
        kernel,
        out_shape=pltpu.VMEM(forcing.shape, F32),
        in_specs=[any_space] * 6,
        out_specs=pl.BlockSpec(memory_space=pltpu.VMEM),
        scratch_shapes=[
            vmem(3, C, C), vmem(C, C), vmem(4, C, C), vmem(16, C, C), vmem(C, C),
            vmem(3, W, C), vmem(5, *field), vmem(3, 13, W, C),
            vmem(12, C + 16, C), vmem(C, C), vmem(4, C, C), vmem(4, C, C),
            *(vmem(4, *field) for _ in range(5)), vmem(3, *field),
            vmem(*field), vmem(*field), vmem(*field),
            vmem(*field), vmem(W, C), vmem(*field), vmem(*field), vmem(C, C),
            vmem(*field), vmem(*field), vmem(*field),
            vmem(2, 2 * H, C), vmem(C - 32, C), vmem(40, C), vmem(40, C), vmem(2 * H, C), vmem(2 * H, C),
            vmem(2 * H, C), vmem(2 * H, C), vmem(H, C), vmem(H, C), vmem(W, C),
            vmem(3, 24, C), vmem(3, 24, C), *(vmem(6, 8, C) for _ in range(4)),
            pltpu.SemaphoreType.DMA((6,)),
            pltpu.SemaphoreType.DMA((28,)),
            pltpu.SemaphoreType.DMA((28,)),
            pltpu.SemaphoreType.DMA((4,)),
            pltpu.SemaphoreType.DMA((4,)),
        ],
        compiler_params=pltpu.CompilerParams(collective_id=0, has_side_effects=True, vmem_limit_bytes=60 << 20),
    )(u_init, guess, forcing, speed_x, speed_y, diffusion)


def solution(mesh):
    placed = (
        P(None, "sy"),
        P(("tm", "sx"), None, "sy"),
        P(("tm", "sx"), None, "sy"),
        P(None, "sy"),
        P(None, "sy"),
        P(None, "sy"),
    )
    return jax.shard_map(
        local, mesh=mesh, in_specs=placed, out_specs=P(("tm", "sx"), None, "sy"), check_vma=False
    )
```

```python
import functools

import jax
import jax.numpy as jnp
from jax import lax
from jax.experimental import pallas as pl
from jax.experimental.pallas import tpu as pltpu
from jax.sharding import PartitionSpec as P

MESH = pl.DeviceIdType.MESH
C = 128
H = 16
W = C + 2 * H
Z = 8
N = W + 2 * Z
F32 = jnp.float32


def west_of(x):
    return pltpu.roll(x, 1, 1)


def east_of(x):
    return pltpu.roll(x, C - 1, 1)


def build(base, coef, lo, n):
    def at(j, shift):
        return base[j, pl.ds(lo + shift, n), :]

    w, e, s, n_, c = (at(j, 0) for j in range(5))
    ww, we, ws, wn, wc = (west_of(x) for x in (w, e, s, n_, c))
    ew, ee, es, en, ec = (east_of(x) for x in (w, e, s, n_, c))
    loop = (w * we + e * ew) + (s * at(3, -1) + n_ * at(2, 1))
    centre = 0.5 * (c * c + loop)
    to_west = -0.5 * w * (c + wc)
    to_east = -0.5 * e * (c + ec)
    to_south = -0.5 * s * (c + at(4, -1))
    to_north = -0.5 * n_ * (c + at(4, 1))
    west_south = 0.5 * (w * ws + s * at(0, -1))
    west_north = 0.5 * (w * wn + n_ * at(0, 1))
    east_south = 0.5 * (e * es + s * at(1, -1))
    east_north = 0.5 * (e * en + n_ * at(1, 1))
    linear = (-c, s, n_, ew, we)
    square = (centre, to_south, to_north, east_of(to_west), west_of(to_east))
    rest = (0.5 * s * at(2, -1), 0.5 * n_ * at(3, 1), 0.5 * w * ww, 0.5 * e * ee,
            east_of(west_south), east_of(west_north), west_of(east_south), west_of(east_north))
    rows = pl.ds(lo - Z, n)
    for m, factor in enumerate((1.0, 4.0, 16.0)):
        for j in range(5):
            term = factor * linear[j] + (factor * factor) * square[j]
            coef[m, j, rows, :] = 1.0 + term if j == 0 else term
        for j in range(8):
            coef[m, 5 + j, rows, :] = (factor * factor) * rest[j]


def heun(coef, m, src, at, lo, n):
    def field(shift):
        return src[at + (pl.ds(lo + shift, n),)]

    def k(j):
        return coef[m, j, pl.ds(lo - Z, n), :]

    v, south, north = field(0), field(-1), field(1)
    from_west = k(3) * v + k(9) * south + k(10) * north
    from_east = k(4) * v + k(11) * south + k(12) * north
    columns = (k(0) * v + k(1) * south) + (k(2) * north + k(5) * field(-2)) + k(6) * field(2)
    rows = k(7) * pltpu.roll(v, 2, 1) + k(8) * pltpu.roll(v, C - 2, 1)
    return (columns + rows) + (west_of(from_west) + east_of(from_east))


def kernel(u_hbm, guess_hbm, forcing_hbm, sx_hbm, sy_hbm, d_hbm, out,
           raw_k, raw_u, raw_g, raw_f, prev, kraw, base, coef, hold, g3, f2, f3, sa, sb, sc, sd, rp, rf,
           la, lb, lc, y1p, y1, y2, y1f, y2f, e1p, e1, bf, handed, em, em_low, em_high, el, er, rl, rr, rl2, rr2, yl, rsl, rsr, to_left, to_right, from_left, from_right,
           lsem, ssem, rsem, k_sem, e_sem):
    tm, sx, c = lax.axis_index("tm"), lax.axis_index("sx"), lax.axis_index("sy")
    count = lax.axis_size("sy")
    place = 2 * tm + sx
    has_left, has_right = c > 0, c < count - 1
    left, right = lax.rem(c + count - 1, count), lax.rem(c + 1, count)

    def fetch(src, dst, i):
        copy = pltpu.make_async_copy(src, dst, lsem.at[i])
        copy.start()
        return copy

    loads_k = [fetch(ref, raw_k.at[i], i) for i, ref in enumerate((sx_hbm, sy_hbm, d_hbm))]
    load_g = fetch(guess_hbm, raw_g, 3)
    load_u = fetch(u_hbm, raw_u, 4)
    load_f = fetch(forcing_hbm, raw_f, 5)

    teller = (tm == 1) | (sx == 0)
    barrier = pltpu.get_barrier_semaphore()

    def greet(*device):
        pl.semaphore_signal(barrier, inc=1, device_id=device, device_id_type=MESH)

    @pl.when(has_left)
    def _():
        greet(tm, tm * sx, left)

    @pl.when(has_right)
    def _():
        greet(tm, tm * sx, right)

    greet(tm, 1 - sx, c)

    @pl.when(tm == 1)
    def _():
        greet(0, 0, c)
        greet(0, 1, c)

    for ref in (sa, sb, sc, sd, rp, rf, la, lb, lc, bf, base, e1p):
        ref[...] = jnp.zeros_like(ref)
    for ref in (y1p, y1f, y2, e1p, e1):
        ref[pl.ds(0, Z), :] = jnp.zeros((Z, ref.shape[1]), F32)
        ref[pl.ds(N - Z, Z), :] = jnp.zeros((Z, ref.shape[1]), F32)

    hold[:, pl.ds(0, 8), :] = jnp.zeros((12, 8, C), F32)
    hold[:, pl.ds(8 + C, 8), :] = jnp.zeros((12, 8, C), F32)

    @pl.when(c == 0)
    def _():
        kraw[:, pl.ds(0, H), :] = jnp.zeros((3, H, C), F32)
        from_left[...] = jnp.zeros_like(from_left)
        rl[...] = jnp.zeros_like(rl)
        rsl[...] = jnp.zeros_like(rsl)
        el[...] = jnp.zeros_like(el)

    @pl.when(c == count - 1)
    def _():
        kraw[:, pl.ds(H + C, H), :] = jnp.zeros((3, H, C), F32)
        from_right[...] = jnp.zeros_like(from_right)
        rr[...] = jnp.zeros_like(rr)
        rsr[...] = jnp.zeros_like(rsr)
        er[...] = jnp.zeros_like(er)

    for i, load in enumerate(loads_k):
        load.wait()
        kraw[i, pl.ds(H, C), :] = raw_k[i].T

    sides = jnp.where(has_left, 1, 0) + jnp.where(has_right, 1, 0)
    pl.semaphore_wait(barrier, 1 + jnp.where(tm == 0, 2 + 2 * (1 - sx) * sides, sides))

    sent = []

    def make_copy(src, dst, send_sem, recv_sem, *device):
        return pltpu.make_async_remote_copy(src_ref=src, dst_ref=dst, send_sem=send_sem, recv_sem=recv_sem,
                                            device_id=device, device_id_type=MESH)

    def copy_of(i, src, dst, *device, at=None):
        return make_copy(src, dst, ssem.at[i], rsem.at[i if at is None else at], *device)

    def pair(i, to_right, at_right, to_left, at_left):
        sent.append((copy_of(i, to_right, at_right, tm, sx, right), copy_of(i + 1, to_left, at_left, tm, sx, left)))
        return sent[-1]

    def tell(copies):
        pl.when(has_right)(copies[0].start)
        pl.when(has_left)(copies[1].start)

    def both(*what):
        copies = pair(*what)
        tell(copies)
        return copies

    def arrive(up, down):
        pl.when(has_left)(up.wait_recv)
        pl.when(has_right)(down.wait_recv)

    halo_k = []
    for i, to, told in ((0, tm * sx, teller), (2, 1, place == 0)):
        up = make_copy(kraw.at[:, pl.ds(C, H), :], kraw.at[:, pl.ds(0, H), :], k_sem.at[i], rsem.at[0], tm, to, right)
        down = make_copy(kraw.at[:, pl.ds(H, H), :], kraw.at[:, pl.ds(H + C, H), :], k_sem.at[i + 1], rsem.at[1],
                         tm, to, left)
        pl.when(told & has_right)(up.start)
        pl.when(told & has_left)(down.start)
        halo_k.append((up, down, told))

    load_g.wait()
    after = place + 1
    onward = (lax.div(after, 2), lax.rem(after, 2), c)
    prev_copy = copy_of(2, raw_g.at[3], prev, *onward)

    @pl.when(place < 3)
    def _():
        prev_copy.start()

    for i in range(3):
        hold[1 + i, pl.ds(8, C), :] = raw_g[i].T
    g3[...] = raw_g[3].T
    load_u.wait()
    load_f.wait()
    for j in range(4):
        hold[4 + j, pl.ds(8, C), :] = raw_f[4 * j].T
        hold[8 + j, pl.ds(8, C), :] = raw_f[4 * j + 1].T
    for i in range(4):
        to_right[i, pl.ds(6, 2), :] = hold[8 + i, pl.ds(8 + C - 2, 2), :]
        to_left[i, pl.ds(6, 2), :] = hold[8 + i, pl.ds(8, 2), :]
        to_right[4 + i // 2, pl.ds(4 * (i % 2), 4), :] = hold[4 + i, pl.ds(8 + C - 4, 4), :]
        to_left[4 + i // 2, pl.ds(4 * (i % 2), 4), :] = hold[4 + i, pl.ds(8, 4), :]
    for i in range(1, 4):
        to_right[i, pl.ds(0, 6), :] = hold[i, pl.ds(8 + C - 6, 6), :]
        to_left[i, pl.ds(0, 6), :] = hold[i, pl.ds(8, 6), :]
    tiles = pl.ds(1, 5)
    halo_h = pair(3, to_right.at[tiles], from_left.at[tiles], to_left.at[tiles], from_right.at[tiles])
    halo_s = pair(5, to_right.at[0], from_left.at[0], to_left.at[0], from_right.at[0])
    early = place != 1
    pl.when(early)(lambda: tell(halo_h))
    for j in range(4):
        f2[j] = raw_f[4 * j + 2].T
        f3[j] = raw_f[4 * j + 3].T

    def differences(lo, n):
        x, y, diffusion = (kraw[i, pl.ds(lo - Z, n), :] for i in range(3))
        row = lax.broadcasted_iota(jnp.int32, (n, C), 1)
        west = jnp.maximum(x, 0.0) + diffusion
        east = diffusion - jnp.minimum(x, 0.0)
        south = jnp.maximum(y, 0.0) + diffusion
        north = diffusion - jnp.minimum(y, 0.0)
        rows = pl.ds(lo, n)
        base[0, rows, :] = jnp.where(row == 0, 0.0, west)
        base[1, rows, :] = jnp.where(row == C - 1, 0.0, east)
        base[2, rows, :] = south
        base[3, rows, :] = north
        base[4, rows, :] = (west + east) + (south + north)

    first = Z + H
    main = pl.ds(first, C)
    span = pl.ds(Z, W)
    fields = [(i,) for i in range(4)]
    differences(first, C)
    for j in range(4):
        build(base, coef, first + 32 * j, 32)

    def source(level, i, col, n):
        if level < 2:
            return hold[4 + 4 * level + i, pl.ds(8 + col, n), :]
        if level == 2:
            return f2[i, pl.ds(col, n), :]
        at_end = hold[1 + i, pl.ds(8 + col, n), :] if i < 3 else g3[pl.ds(col, n), :]
        return f3[i, pl.ds(col, n), :] - at_end

    levels = (sa, sb, sc, sd, rp)
    def relax_inner(which):
        for i in which:
            sa[i, main, :] = hold[i, pl.ds(8, C), :]
        for level in range(4):
            for col in (0, 64):
                for i in which:
                    levels[level + 1][i, pl.ds(first + col, 64), :] = (
                        heun(coef, 0, levels[level], (i,), first + col, 64) + source(level, i, col, 64))

    relax_inner((1, 2, 3))

    @pl.when(place == 0)
    def _():
        hold[0, pl.ds(8, C), :] = raw_u[...].T

    @pl.when(place > 0)
    def _():
        prev_copy.wait_recv()
        hold[0, pl.ds(8, C), :] = prev[...].T

    to_right[0, pl.ds(0, 6), :] = hold[0, pl.ds(8 + C - 6, 6), :]
    to_left[0, pl.ds(0, 6), :] = hold[0, pl.ds(8, 6), :]
    pl.when(early)(lambda: tell(halo_s))

    relax_inner((0,))

    def single(m, src, at, dst, term, parts):
        for lo, n in parts:
            dst[pl.ds(lo, n), :] = heun(coef, m, src, at, lo, n) + term(lo, n)

    def rows_of(ref, *at):
        return lambda lo, n: ref[at + (pl.ds(lo, n),)]

    def right_side(parts):
        single(1, rp, (0,), la, rows_of(rp, 1), parts)
        single(1, la, (), lb, rows_of(rp, 2), parts)
        single(1, lb, (), y2, rows_of(rp, 3), parts)

    inner = [(first + 32 * j, 32) for j in range(4)]
    whole = [(Z + 32 * j, 32) for j in range(5)]
    right_side(inner)

    core = pl.ds(first + 16, C - 32)
    sides_of = (pl.ds(Z, 2 * H), pl.ds(Z + C, 2 * H))
    hand_in = copy_of(9, y2.at[core, :], y1p.at[core, :], tm, 1, c)
    hand_out = [copy_of(22 + i, y2.at[rows, :], handed.at[i], tm, 1, c) for i, rows in enumerate(sides_of)]
    cross_in = copy_of(14, e1p.at[core, :], em, 1, 1, c)
    relay = copy_of(15, em, em, 1, 0, c, at=14)
    low, high = pl.ds(Z, 40), pl.ds(Z + W - 40, 40)
    cross_out, cross_sides = [], []
    for s in (1, 0):
        cross_sides.append((copy_of(16 + s, e1p.at[pl.ds(Z + C, 2 * H), :], el, 1, s, right, at=16),
                            copy_of(18 + s, e1p.at[pl.ds(Z, 2 * H), :], er, 1, s, left, at=17)))
        cross_out.append((copy_of(24 + s, e1p.at[low, :], em_low, 1, s, c, at=24),
                          copy_of(26 + s, e1p.at[high, :], em_high, 1, s, c, at=25)))

    pl.when(sx == 0)(hand_in.start)
    pl.when(place == 1)(hand_in.wait_recv)

    @pl.when(place == 1)
    def _():
        single(2, y1p, (), e1p, rows_of(y2), [(first + 16, 48), (first + 64, 48)])
        cross_in.start()

    arrive(*halo_k[0][:2])

    @pl.when(place == 1)
    def _():
        tell(halo_h)
        tell(halo_s)

    differences(Z, H)
    differences(first + C, H)
    build(base, coef, Z, 24)
    build(base, coef, first + C - 8, 24)
    for level in range(4):
        for (i,) in fields:
            x = heun(coef, 0, levels[level], (i,), first - 8, 16)
            levels[level + 1][i, pl.ds(first - 8, 8), :] = x[:8]
            levels[level + 1][i, pl.ds(first, 8), :] = x[8:] + source(level, i, 0, 8)
            x = heun(coef, 0, levels[level], (i,), first + C - 8, 16)
            levels[level + 1][i, pl.ds(first + C - 8, 8), :] = x[:8] + source(level, i, C - 8, 8)
            levels[level + 1][i, pl.ds(first + C, 8), :] = x[8:]

    halo_r = both(7, rp.at[0, pl.ds(Z + C, 24), :], rsl.at[0], rp.at[0, pl.ds(Z + H - 8, 24), :], rsr.at[0])
    halo_t = both(20, rp.at[pl.ds(1, 2), pl.ds(Z + C + 8, 16), :], rsl.at[pl.ds(1, 2), pl.ds(8, 16), :],
                  rp.at[pl.ds(1, 2), pl.ds(Z + H - 8, 16), :], rsr.at[pl.ds(1, 2), pl.ds(0, 16), :])

    right_side([(Z, 2 * H), (Z + C, 2 * H)])


    edge_1 = []
    for to in range(2):
        edge_1.append((make_copy(y2.at[pl.ds(Z + C, 2 * H), :], rl, e_sem.at[2 * to], rsem.at[10], tm, to, right),
                       make_copy(y2.at[pl.ds(Z, 2 * H), :], rr, e_sem.at[2 * to + 1], rsem.at[11], tm, to, left)))

    @pl.when(sx == 0)
    def _():
        for to in (1, 0):
            tell(edge_1[to])
        for copy in hand_out:
            copy.start()
        y1[...] = y2[span, :]

    @pl.when(sx == 1)
    def _():
        pl.when(tm == 1)(hand_in.wait_recv)
        for i, copy in enumerate(hand_out):
            copy.wait_recv()
            y1p[sides_of[i], :] = handed[i]
        y1[...] = y1p[span, :]

    @pl.when(place == 1)
    def _():
        cross_in.wait_send()
        single(2, y1p, (), e1p, rows_of(y2), [(Z, 40), (Z + W - 40, 40)])
        for (up, down), outer in zip(cross_sides, cross_out):
            for copy in outer:
                copy.start()
            pl.when(has_right)(up.start)
            pl.when(has_left)(down.start)
        yl[...] = e1p[span, :]

    @pl.when(place != 1)
    def _():
        yl[...] = y2[span, :]

    edge_2 = pair(12, yl.at[pl.ds(H + C, H), :], rl2, yl.at[pl.ds(0, H), :], rr2)
    pl.when(sx == 1)(lambda: tell(edge_2))

    def joined(dst, own, from_left, from_right, middle=True):
        dst[pl.ds(Z, 2 * H), :] = own[pl.ds(0, 2 * H), :] + from_left[...]
        dst[pl.ds(Z + C, 2 * H), :] = own[pl.ds(C, 2 * H), :] + from_right[...]
        if middle:
            dst[pl.ds(Z + 2 * H, C - 2 * H), :] = own[pl.ds(2 * H, C - 2 * H), :]

    y1f[pl.ds(Z + 2 * H, C - 2 * H), :] = y1[pl.ds(2 * H, C - 2 * H), :]
    y2f[pl.ds(H, C - 2 * H), :] = yl[pl.ds(2 * H, C - 2 * H), :]
    for i in range(3):
        rf[i, pl.ds(Z + 24, W - 48), :] = rp[i, pl.ds(Z + 24, W - 48), :]

    def sums():
        joined(y1f, y1, rl, rr, False)
        for i in range(3):
            if i == 0:
                rf[i, pl.ds(Z, 24), :] = rp[i, pl.ds(Z, 24), :] + rsl[i]
                rf[i, pl.ds(Z + W - 24, 24), :] = rp[i, pl.ds(Z + W - 24, 24), :] + rsr[i]
            else:
                rf[i, pl.ds(Z + 8, 16), :] = rp[i, pl.ds(Z + 8, 16), :] + rsl[i, pl.ds(8, 16), :]
                rf[i, pl.ds(Z + W - 24, 16), :] = rp[i, pl.ds(Z + W - 24, 16), :] + rsr[i, pl.ds(0, 16), :]

    later = tm == 1
    pl.when(later)(cross_in.wait_recv)
    pl.when(place == 3)(relay.start)

    @pl.when(place == 1)
    def _():
        bf[span, :] = y1p[span, :]

    @pl.when(place == 2)
    def _():
        bf[core, :] = em[...]

    @pl.when(place == 3)
    def _():
        e1[core, :] = em[...]
        single(2, e1, (), bf, rows_of(y1p), inner)

    chain = ((bf, la), (la, lb), (lb, lc))
    starts = (bf, la, lb, lc)

    for i, (src, dst) in enumerate(chain):
        single(1, src, (), dst, rows_of(rp, i), inner)
    for (i,) in fields:
        sa[i, main, :] = hold[i, pl.ds(8, C), :] + starts[i][main, :]
    for level in range(3):
        for col in (0, 64):
            for (i,) in fields:
                levels[level + 1][i, pl.ds(first + col, 64), :] = (
                    heun(coef, 0, levels[level], (i,), first + col, 64) + source(level, i, col, 64))

    for copies in (edge_1[0], halo_r, halo_t, halo_h, halo_s):
        arrive(*copies)
    sums()
    for i in range(4):
        hold[i, pl.ds(2, 6), :] = from_left[i, pl.ds(0, 6), :]
        hold[i, pl.ds(8 + C, 6), :] = from_right[i, pl.ds(0, 6), :]
        hold[4 + i, pl.ds(4, 4), :] = from_left[4 + i // 2, pl.ds(4 * (i % 2), 4), :]
        hold[4 + i, pl.ds(8 + C, 4), :] = from_right[4 + i // 2, pl.ds(4 * (i % 2), 4), :]
        hold[8 + i, pl.ds(6, 2), :] = from_left[i, pl.ds(6, 2), :]
        hold[8 + i, pl.ds(8 + C, 2), :] = from_right[i, pl.ds(6, 2), :]
    @pl.when(later)
    def _():
        for copy in cross_out[0]:
            copy.wait_recv()

    pl.when(later & has_left)(cross_sides[0][0].wait_recv)
    pl.when(later & has_right)(cross_sides[0][1].wait_recv)

    edges = [(Z, 48), (Z + W - 48, 48)]

    def crossed(dst):
        dst[pl.ds(Z, 2 * H), :] = em_low[pl.ds(0, 2 * H), :] + el[...]
        dst[pl.ds(Z + 2 * H, 8), :] = em_low[pl.ds(2 * H, 8), :]
        dst[pl.ds(Z + C - 8, 8), :] = em_high[pl.ds(0, 8), :]
        dst[pl.ds(Z + C, 2 * H), :] = em_high[pl.ds(8, 2 * H), :] + er[...]

    @pl.when(place == 1)
    def _():
        bf[span, :] = y1f[span, :]

    @pl.when(place == 2)
    def _():
        crossed(bf)


    @pl.when(place == 3)
    def _():
        crossed(e1)
        single(2, e1, (), bf, rows_of(y1f), edges)

    def correct(i):
        src, dst = chain[i]
        single(1, src, (), dst, rows_of(rf, i), edges)

    def begin(i):
        for lo in (first - 8, first + C - 32):
            sa[i, pl.ds(lo, 40), :] = hold[i, pl.ds(lo - first + 8, 40), :] + starts[i][pl.ds(lo, 40), :]
        if i:
            out[4 * i - 1] = sa[i, main, :]

    def relax(i, level):
        for lo, n in ((first - 8, 40), (first + C - 32, 40)) if level < 2 else ((first, 32), (first + C - 32, 32)):
            levels[level + 1][i, pl.ds(lo, n), :] = (
                heun(coef, 0, levels[level], (i,), lo, n) + source(level, i, lo - first, n))
        out[4 * i + level] = levels[level + 1][i, main, :]

    begin(0)
    correct(0)
    relax(0, 0)
    begin(1)
    correct(1)
    relax(0, 1)
    relax(1, 0)
    begin(2)
    correct(2)
    relax(0, 2)
    relax(1, 1)
    relax(2, 0)
    begin(3)
    relax(1, 2)
    relax(2, 1)
    relax(3, 0)
    relax(2, 2)
    relax(3, 1)
    relax(3, 2)
    pl.when(sx == 1)(lambda: arrive(*edge_2))

    @pl.when((sx == 0) | (c == 0))
    def _():
        rl2[...] = jnp.zeros_like(rl2)

    @pl.when((sx == 0) | (c == count - 1))
    def _():
        rr2[...] = jnp.zeros_like(rr2)

    y2f[pl.ds(0, H), :] = yl[pl.ds(H, H), :] + rl2[...]
    y2f[pl.ds(C - H, H), :] = yl[pl.ds(C, H), :] + rr2[...]
    right_after = jnp.where(sx == 0, y1f[main, :], y2f[...])
    own = jnp.concatenate([heun(coef, 2, bf, (), lo, n) for lo, n in inner], 0)
    out[15] = g3[...] + (right_after + jnp.where(place == 1, 0.0, own))

    for up, down in sent:
        told = sx == 1 if up is edge_2[0] else True
        pl.when(told & has_right)(up.wait_send)
        pl.when(told & has_left)(down.wait_send)
    for up, down, told in halo_k + [copies + (sx == 0,) for copies in edge_1]:
        pl.when(told & has_right)(up.wait_send)
        pl.when(told & has_left)(down.wait_send)

    @pl.when(place < 3)
    def _():
        prev_copy.wait_send()

    @pl.when(sx == 0)
    def _():
        hand_in.wait_send()
        for copy in hand_out:
            copy.wait_send()

    @pl.when(place == 1)
    def _():
        for copy in cross_out[0] + cross_out[1]:
            copy.wait_send()
        for up, down in cross_sides:
            pl.when(has_right)(up.wait_send)
            pl.when(has_left)(down.wait_send)

    pl.when(place == 3)(relay.wait_send)


def local(u_init, guess, forcing, speed_x, speed_y, diffusion):
    def vmem(*shape):
        return pltpu.VMEM(shape, F32)

    any_space = pl.BlockSpec(memory_space=pltpu.HBM)
    field = (N, C)
    by_column = pl.pallas_call(
        kernel,
        out_shape=pltpu.VMEM(forcing.shape, F32),
        in_specs=[any_space] * 6,
        out_specs=pl.BlockSpec(memory_space=pltpu.VMEM),
        scratch_shapes=[
            vmem(3, C, C), vmem(C, C), vmem(4, C, C), vmem(16, C, C), vmem(C, C),
            vmem(3, W, C), vmem(5, *field), vmem(3, 13, W, C),
            vmem(12, C + 16, C), vmem(C, C), vmem(4, C, C), vmem(4, C, C),
            *(vmem(4, *field) for _ in range(5)), vmem(3, *field),
            vmem(*field), vmem(*field), vmem(*field),
            vmem(*field), vmem(W, C), vmem(*field), vmem(*field), vmem(C, C),
            vmem(*field), vmem(*field), vmem(*field),
            vmem(2, 2 * H, C), vmem(C - 32, C), vmem(40, C), vmem(40, C), vmem(2 * H, C), vmem(2 * H, C),
            vmem(2 * H, C), vmem(2 * H, C), vmem(H, C), vmem(H, C), vmem(W, C),
            vmem(3, 24, C), vmem(3, 24, C), *(vmem(6, 8, C) for _ in range(4)),
            pltpu.SemaphoreType.DMA((6,)),
            pltpu.SemaphoreType.DMA((28,)),
            pltpu.SemaphoreType.DMA((28,)),
            pltpu.SemaphoreType.DMA((4,)),
            pltpu.SemaphoreType.DMA((4,)),
        ],
        compiler_params=pltpu.CompilerParams(collective_id=0, has_side_effects=True, vmem_limit_bytes=60 << 20),
    )(u_init, guess, forcing, speed_x, speed_y, diffusion)
    return jnp.swapaxes(by_column, 1, 2)


def solution(mesh):
    placed = (
        P(None, "sy"),
        P(("tm", "sx"), None, "sy"),
        P(("tm", "sx"), None, "sy"),
        P(None, "sy"),
        P(None, "sy"),
        P(None, "sy"),
    )
    return jax.shard_map(
        local, mesh=mesh, in_specs=placed, out_specs=P(("tm", "sx"), None, "sy"), check_vma=False
    )
```

```python
import functools

import jax
import jax.numpy as jnp
from jax import lax
from jax.experimental import pallas as pl
from jax.experimental.pallas import tpu as pltpu
from jax.sharding import PartitionSpec as P

MESH = pl.DeviceIdType.MESH
C = 128
H = 16
W = C + 2 * H
Z = 8
N = W + 2 * Z
F32 = jnp.float32


def west_of(x):
    return pltpu.roll(x, 1, 1)


def east_of(x):
    return pltpu.roll(x, C - 1, 1)


def build(base, coef, lo, n):
    def at(j, shift):
        return base[j, pl.ds(lo + shift, n), :]

    w, e, s, n_, c = (at(j, 0) for j in range(5))
    ww, we, ws, wn, wc = (west_of(x) for x in (w, e, s, n_, c))
    ew, ee, es, en, ec = (east_of(x) for x in (w, e, s, n_, c))
    loop = (w * we + e * ew) + (s * at(3, -1) + n_ * at(2, 1))
    centre = 0.5 * (c * c + loop)
    to_west = -0.5 * w * (c + wc)
    to_east = -0.5 * e * (c + ec)
    to_south = -0.5 * s * (c + at(4, -1))
    to_north = -0.5 * n_ * (c + at(4, 1))
    west_south = 0.5 * (w * ws + s * at(0, -1))
    west_north = 0.5 * (w * wn + n_ * at(0, 1))
    east_south = 0.5 * (e * es + s * at(1, -1))
    east_north = 0.5 * (e * en + n_ * at(1, 1))
    linear = (-c, s, n_, ew, we)
    square = (centre, to_south, to_north, east_of(to_west), west_of(to_east))
    rest = (0.5 * s * at(2, -1), 0.5 * n_ * at(3, 1), 0.5 * w * ww, 0.5 * e * ee,
            east_of(west_south), east_of(west_north), west_of(east_south), west_of(east_north))
    rows = pl.ds(lo - Z, n)
    for m, factor in enumerate((1.0, 4.0, 16.0)):
        for j in range(5):
            term = factor * linear[j] + (factor * factor) * square[j]
            coef[m, j, rows, :] = 1.0 + term if j == 0 else term
        for j in range(8):
            coef[m, 5 + j, rows, :] = (factor * factor) * rest[j]


def heun(coef, m, src, at, lo, n):
    def field(shift):
        return src[at + (pl.ds(lo + shift, n),)]

    def k(j):
        return coef[m, j, pl.ds(lo - Z, n), :]

    v, south, north = field(0), field(-1), field(1)
    from_west = k(3) * v + k(9) * south + k(10) * north
    from_east = k(4) * v + k(11) * south + k(12) * north
    columns = (k(0) * v + k(1) * south) + (k(2) * north + k(5) * field(-2)) + k(6) * field(2)
    rows = k(7) * pltpu.roll(v, 2, 1) + k(8) * pltpu.roll(v, C - 2, 1)
    return (columns + rows) + (west_of(from_west) + east_of(from_east))


def kernel(u_hbm, guess_hbm, forcing_hbm, sx_hbm, sy_hbm, d_hbm, out,
           raw_k, raw_u, raw_g, raw_f, prev, kraw, base, coef, hold, g3, f2, f3, sa, sb, sc, sd, rp, rf,
           la, lb, lc, y1p, y1, y2, y1f, y2f, e1p, e1, bf, handed, em, em_low, em_high, el, er, rl, rr, rl2, rr2, yl, rsl, rsr, to_left, to_right, from_left, from_right,
           lsem, ssem, rsem, k_sem, e_sem):
    tm, sx, c = lax.axis_index("tm"), lax.axis_index("sx"), lax.axis_index("sy")
    count = lax.axis_size("sy")
    place = 2 * tm + sx
    has_left, has_right = c > 0, c < count - 1
    left, right = lax.rem(c + count - 1, count), lax.rem(c + 1, count)

    def fetch(src, dst, i):
        copy = pltpu.make_async_copy(src, dst, lsem.at[i])
        copy.start()
        return copy

    loads_k = [fetch(ref, raw_k.at[i], i) for i, ref in enumerate((sx_hbm, sy_hbm, d_hbm))]
    load_g = fetch(guess_hbm, raw_g, 3)
    load_u = fetch(u_hbm, raw_u, 4)
    load_f = fetch(forcing_hbm, raw_f, 5)

    teller = (tm == 1) | (sx == 0)
    barrier = pltpu.get_barrier_semaphore()

    def greet(*device):
        pl.semaphore_signal(barrier, inc=1, device_id=device, device_id_type=MESH)

    @pl.when(has_left)
    def _():
        greet(tm, tm * sx, left)

    @pl.when(has_right)
    def _():
        greet(tm, tm * sx, right)

    greet(tm, 1 - sx, c)

    @pl.when(tm == 1)
    def _():
        greet(0, 0, c)
        greet(0, 1, c)

    for ref in (sa, sb, sc, sd, rp, rf, la, lb, lc, bf, base, e1p):
        ref[...] = jnp.zeros_like(ref)
    for ref in (y1p, y1f, y2, e1p, e1):
        ref[pl.ds(0, Z), :] = jnp.zeros((Z, ref.shape[1]), F32)
        ref[pl.ds(N - Z, Z), :] = jnp.zeros((Z, ref.shape[1]), F32)

    hold[:, pl.ds(0, 8), :] = jnp.zeros((12, 8, C), F32)
    hold[:, pl.ds(8 + C, 8), :] = jnp.zeros((12, 8, C), F32)

    @pl.when(c == 0)
    def _():
        kraw[:, pl.ds(0, H), :] = jnp.zeros((3, H, C), F32)
        from_left[...] = jnp.zeros_like(from_left)
        rl[...] = jnp.zeros_like(rl)
        rsl[...] = jnp.zeros_like(rsl)
        el[...] = jnp.zeros_like(el)

    @pl.when(c == count - 1)
    def _():
        kraw[:, pl.ds(H + C, H), :] = jnp.zeros((3, H, C), F32)
        from_right[...] = jnp.zeros_like(from_right)
        rr[...] = jnp.zeros_like(rr)
        rsr[...] = jnp.zeros_like(rsr)
        er[...] = jnp.zeros_like(er)

    for i, load in enumerate(loads_k):
        load.wait()
        kraw[i, pl.ds(H, C), :] = raw_k[i].T

    sides = jnp.where(has_left, 1, 0) + jnp.where(has_right, 1, 0)
    pl.semaphore_wait(barrier, 1 + jnp.where(tm == 0, 2 + 2 * (1 - sx) * sides, sides))

    sent = []

    def make_copy(src, dst, send_sem, recv_sem, *device):
        return pltpu.make_async_remote_copy(src_ref=src, dst_ref=dst, send_sem=send_sem, recv_sem=recv_sem,
                                            device_id=device, device_id_type=MESH)

    def copy_of(i, src, dst, *device, at=None):
        return make_copy(src, dst, ssem.at[i], rsem.at[i if at is None else at], *device)

    def pair(i, to_right, at_right, to_left, at_left):
        sent.append((copy_of(i, to_right, at_right, tm, sx, right), copy_of(i + 1, to_left, at_left, tm, sx, left)))
        return sent[-1]

    def tell(copies):
        pl.when(has_right)(copies[0].start)
        pl.when(has_left)(copies[1].start)

    def both(*what):
        copies = pair(*what)
        tell(copies)
        return copies

    def arrive(up, down):
        pl.when(has_left)(up.wait_recv)
        pl.when(has_right)(down.wait_recv)

    halo_k = []
    for i, to, told in ((0, tm * sx, teller), (2, 1, place == 0)):
        up = make_copy(kraw.at[:, pl.ds(C, H), :], kraw.at[:, pl.ds(0, H), :], k_sem.at[i], rsem.at[0], tm, to, right)
        down = make_copy(kraw.at[:, pl.ds(H, H), :], kraw.at[:, pl.ds(H + C, H), :], k_sem.at[i + 1], rsem.at[1],
                         tm, to, left)
        pl.when(told & has_right)(up.start)
        pl.when(told & has_left)(down.start)
        halo_k.append((up, down, told))

    load_g.wait()
    after = place + 1
    onward = (lax.div(after, 2), lax.rem(after, 2), c)
    prev_copy = copy_of(2, raw_g.at[3], prev, *onward)

    @pl.when(place < 3)
    def _():
        prev_copy.start()

    for i in range(3):
        hold[1 + i, pl.ds(8, C), :] = raw_g[i].T
    g3[...] = raw_g[3].T
    load_u.wait()
    load_f.wait()
    for j in range(4):
        hold[4 + j, pl.ds(8, C), :] = raw_f[4 * j].T
        hold[8 + j, pl.ds(8, C), :] = raw_f[4 * j + 1].T
    for i in range(4):
        to_right[i, pl.ds(6, 2), :] = hold[8 + i, pl.ds(8 + C - 2, 2), :]
        to_left[i, pl.ds(6, 2), :] = hold[8 + i, pl.ds(8, 2), :]
        to_right[4 + i // 2, pl.ds(4 * (i % 2), 4), :] = hold[4 + i, pl.ds(8 + C - 4, 4), :]
        to_left[4 + i // 2, pl.ds(4 * (i % 2), 4), :] = hold[4 + i, pl.ds(8, 4), :]
    for i in range(1, 4):
        to_right[i, pl.ds(0, 6), :] = hold[i, pl.ds(8 + C - 6, 6), :]
        to_left[i, pl.ds(0, 6), :] = hold[i, pl.ds(8, 6), :]
    tiles = pl.ds(1, 5)
    halo_h = pair(3, to_right.at[tiles], from_left.at[tiles], to_left.at[tiles], from_right.at[tiles])
    halo_s = pair(5, to_right.at[0], from_left.at[0], to_left.at[0], from_right.at[0])
    early = place != 1
    pl.when(early)(lambda: tell(halo_h))
    for j in range(4):
        f2[j] = raw_f[4 * j + 2].T
        f3[j] = raw_f[4 * j + 3].T

    def differences(lo, n):
        x, y, diffusion = (kraw[i, pl.ds(lo - Z, n), :] for i in range(3))
        row = lax.broadcasted_iota(jnp.int32, (n, C), 1)
        west = jnp.maximum(x, 0.0) + diffusion
        east = diffusion - jnp.minimum(x, 0.0)
        south = jnp.maximum(y, 0.0) + diffusion
        north = diffusion - jnp.minimum(y, 0.0)
        rows = pl.ds(lo, n)
        base[0, rows, :] = jnp.where(row == 0, 0.0, west)
        base[1, rows, :] = jnp.where(row == C - 1, 0.0, east)
        base[2, rows, :] = south
        base[3, rows, :] = north
        base[4, rows, :] = (west + east) + (south + north)

    first = Z + H
    main = pl.ds(first, C)
    span = pl.ds(Z, W)
    fields = [(i,) for i in range(4)]
    differences(first, C)
    for j in range(4):
        build(base, coef, first + 32 * j, 32)

    def source(level, i, col, n):
        if level < 2:
            return hold[4 + 4 * level + i, pl.ds(8 + col, n), :]
        if level == 2:
            return f2[i, pl.ds(col, n), :]
        at_end = hold[1 + i, pl.ds(8 + col, n), :] if i < 3 else g3[pl.ds(col, n), :]
        return f3[i, pl.ds(col, n), :] - at_end

    levels = (sa, sb, sc, sd, rp)
    def relax_inner(which):
        for i in which:
            sa[i, main, :] = hold[i, pl.ds(8, C), :]
        for level in range(4):
            for col in (0, 64):
                for i in which:
                    levels[level + 1][i, pl.ds(first + col, 64), :] = (
                        heun(coef, 0, levels[level], (i,), first + col, 64) + source(level, i, col, 64))

    relax_inner((1, 2, 3))

    @pl.when(place == 0)
    def _():
        hold[0, pl.ds(8, C), :] = raw_u[...].T

    @pl.when(place > 0)
    def _():
        prev_copy.wait_recv()
        hold[0, pl.ds(8, C), :] = prev[...].T

    to_right[0, pl.ds(0, 6), :] = hold[0, pl.ds(8 + C - 6, 6), :]
    to_left[0, pl.ds(0, 6), :] = hold[0, pl.ds(8, 6), :]
    pl.when(early)(lambda: tell(halo_s))

    relax_inner((0,))

    def single(m, src, at, dst, term, parts):
        for lo, n in parts:
            dst[pl.ds(lo, n), :] = heun(coef, m, src, at, lo, n) + term(lo, n)

    def rows_of(ref, *at):
        return lambda lo, n: ref[at + (pl.ds(lo, n),)]

    def right_side(parts):
        single(1, rp, (0,), la, rows_of(rp, 1), parts)
        single(1, la, (), lb, rows_of(rp, 2), parts)
        single(1, lb, (), y2, rows_of(rp, 3), parts)

    inner = [(first + 32 * j, 32) for j in range(4)]
    whole = [(Z + 32 * j, 32) for j in range(5)]
    right_side(inner)

    core = pl.ds(first + 16, C - 32)
    sides_of = (pl.ds(Z, 2 * H), pl.ds(Z + C, 2 * H))
    hand_in = copy_of(9, y2.at[core, :], y1p.at[core, :], tm, 1, c)
    hand_out = [copy_of(22 + i, y2.at[rows, :], handed.at[i], tm, 1, c) for i, rows in enumerate(sides_of)]
    cross_in = copy_of(14, e1p.at[core, :], em, 1, 1, c)
    relay = copy_of(15, em, em, 1, 0, c, at=14)
    low, high = pl.ds(Z, 40), pl.ds(Z + W - 40, 40)
    cross_out, cross_sides = [], []
    for s in (1, 0):
        cross_sides.append((copy_of(16 + s, e1p.at[pl.ds(Z + C, 2 * H), :], el, 1, s, right, at=16),
                            copy_of(18 + s, e1p.at[pl.ds(Z, 2 * H), :], er, 1, s, left, at=17)))
        cross_out.append((copy_of(24 + s, e1p.at[low, :], em_low, 1, s, c, at=24),
                          copy_of(26 + s, e1p.at[high, :], em_high, 1, s, c, at=25)))

    pl.when(sx == 0)(hand_in.start)
    pl.when(place == 1)(hand_in.wait_recv)

    @pl.when(place == 1)
    def _():
        single(2, y1p, (), e1p, rows_of(y2), [(first + 16, 48), (first + 64, 48)])
        cross_in.start()

    arrive(*halo_k[0][:2])

    @pl.when(place == 1)
    def _():
        tell(halo_h)
        tell(halo_s)

    differences(Z, H)
    differences(first + C, H)
    build(base, coef, Z, 24)
    build(base, coef, first + C - 8, 24)
    for level in range(4):
        for (i,) in fields:
            x = heun(coef, 0, levels[level], (i,), first - 8, 16)
            levels[level + 1][i, pl.ds(first - 8, 8), :] = x[:8]
            levels[level + 1][i, pl.ds(first, 8), :] = x[8:] + source(level, i, 0, 8)
            x = heun(coef, 0, levels[level], (i,), first + C - 8, 16)
            levels[level + 1][i, pl.ds(first + C - 8, 8), :] = x[:8] + source(level, i, C - 8, 8)
            levels[level + 1][i, pl.ds(first + C, 8), :] = x[8:]

    halo_r = both(7, rp.at[0, pl.ds(Z + C, 24), :], rsl.at[0], rp.at[0, pl.ds(Z + H - 8, 24), :], rsr.at[0])
    halo_t = both(20, rp.at[pl.ds(1, 2), pl.ds(Z + C + 8, 16), :], rsl.at[pl.ds(1, 2), pl.ds(8, 16), :],
                  rp.at[pl.ds(1, 2), pl.ds(Z + H - 8, 16), :], rsr.at[pl.ds(1, 2), pl.ds(0, 16), :])

    right_side([(Z, 2 * H), (Z + C, 2 * H)])


    edge_1 = []
    for to in range(2):
        edge_1.append((make_copy(y2.at[pl.ds(Z + C, 2 * H), :], rl, e_sem.at[2 * to], rsem.at[10], tm, to, right),
                       make_copy(y2.at[pl.ds(Z, 2 * H), :], rr, e_sem.at[2 * to + 1], rsem.at[11], tm, to, left)))

    @pl.when(sx == 0)
    def _():
        for to in (1, 0):
            tell(edge_1[to])
        for copy in hand_out:
            copy.start()
        y1[...] = y2[span, :]

    @pl.when(sx == 1)
    def _():
        pl.when(tm == 1)(hand_in.wait_recv)
        for i, copy in enumerate(hand_out):
            copy.wait_recv()
            y1p[sides_of[i], :] = handed[i]
        y1[...] = y1p[span, :]

    @pl.when(place == 1)
    def _():
        cross_in.wait_send()
        single(2, y1p, (), e1p, rows_of(y2), [(Z, 40), (Z + W - 40, 40)])
        for (up, down), outer in zip(cross_sides, cross_out):
            for copy in outer:
                copy.start()
            pl.when(has_right)(up.start)
            pl.when(has_left)(down.start)
        yl[...] = e1p[span, :]

    @pl.when(place != 1)
    def _():
        yl[...] = y2[span, :]

    edge_2 = pair(12, yl.at[pl.ds(H + C, H), :], rl2, yl.at[pl.ds(0, H), :], rr2)
    pl.when(sx == 1)(lambda: tell(edge_2))

    def joined(dst, own, from_left, from_right, middle=True):
        dst[pl.ds(Z, 2 * H), :] = own[pl.ds(0, 2 * H), :] + from_left[...]
        dst[pl.ds(Z + C, 2 * H), :] = own[pl.ds(C, 2 * H), :] + from_right[...]
        if middle:
            dst[pl.ds(Z + 2 * H, C - 2 * H), :] = own[pl.ds(2 * H, C - 2 * H), :]

    y1f[pl.ds(Z + 2 * H, C - 2 * H), :] = y1[pl.ds(2 * H, C - 2 * H), :]
    y2f[pl.ds(H, C - 2 * H), :] = yl[pl.ds(2 * H, C - 2 * H), :]
    for i in range(3):
        rf[i, pl.ds(Z + 24, W - 48), :] = rp[i, pl.ds(Z + 24, W - 48), :]

    def sums():
        joined(y1f, y1, rl, rr, False)
        for i in range(3):
            if i == 0:
                rf[i, pl.ds(Z, 24), :] = rp[i, pl.ds(Z, 24), :] + rsl[i]
                rf[i, pl.ds(Z + W - 24, 24), :] = rp[i, pl.ds(Z + W - 24, 24), :] + rsr[i]
            else:
                rf[i, pl.ds(Z + 8, 16), :] = rp[i, pl.ds(Z + 8, 16), :] + rsl[i, pl.ds(8, 16), :]
                rf[i, pl.ds(Z + W - 24, 16), :] = rp[i, pl.ds(Z + W - 24, 16), :] + rsr[i, pl.ds(0, 16), :]

    later = tm == 1
    pl.when(later)(cross_in.wait_recv)
    pl.when(place == 3)(relay.start)

    @pl.when(place == 1)
    def _():
        bf[span, :] = y1p[span, :]

    @pl.when(place == 2)
    def _():
        bf[core, :] = em[...]

    @pl.when(place == 3)
    def _():
        e1[core, :] = em[...]
        single(2, e1, (), bf, rows_of(y1p), inner)

    chain = ((bf, la), (la, lb), (lb, lc))
    starts = (bf, la, lb, lc)

    for i, (src, dst) in enumerate(chain):
        single(1, src, (), dst, rows_of(rp, i), inner)
    for (i,) in fields:
        sa[i, main, :] = hold[i, pl.ds(8, C), :] + starts[i][main, :]
    for level in range(3):
        for col in (0, 64):
            for (i,) in fields:
                levels[level + 1][i, pl.ds(first + col, 64), :] = (
                    heun(coef, 0, levels[level], (i,), first + col, 64) + source(level, i, col, 64))

    arrive(*halo_h)
    arrive(*halo_s)
    for i in range(4):
        hold[i, pl.ds(2, 6), :] = from_left[i, pl.ds(0, 6), :]
        hold[i, pl.ds(8 + C, 6), :] = from_right[i, pl.ds(0, 6), :]
        hold[4 + i, pl.ds(4, 4), :] = from_left[4 + i // 2, pl.ds(4 * (i % 2), 4), :]
        hold[4 + i, pl.ds(8 + C, 4), :] = from_right[4 + i // 2, pl.ds(4 * (i % 2), 4), :]
        hold[8 + i, pl.ds(6, 2), :] = from_left[i, pl.ds(6, 2), :]
        hold[8 + i, pl.ds(8 + C, 2), :] = from_right[i, pl.ds(6, 2), :]
    for copies in (halo_r, halo_t, edge_1[0]):
        arrive(*copies)
    sums()
    @pl.when(later)
    def _():
        for copy in cross_out[0]:
            copy.wait_recv()

    pl.when(later & has_left)(cross_sides[0][0].wait_recv)
    pl.when(later & has_right)(cross_sides[0][1].wait_recv)

    edges = [(Z, 48), (Z + W - 48, 48)]

    def crossed(dst):
        dst[pl.ds(Z, 2 * H), :] = em_low[pl.ds(0, 2 * H), :] + el[...]
        dst[pl.ds(Z + 2 * H, 8), :] = em_low[pl.ds(2 * H, 8), :]
        dst[pl.ds(Z + C - 8, 8), :] = em_high[pl.ds(0, 8), :]
        dst[pl.ds(Z + C, 2 * H), :] = em_high[pl.ds(8, 2 * H), :] + er[...]

    @pl.when(place == 1)
    def _():
        bf[span, :] = y1f[span, :]

    @pl.when(place == 2)
    def _():
        crossed(bf)


    @pl.when(place == 3)
    def _():
        crossed(e1)
        single(2, e1, (), bf, rows_of(y1f), edges)

    def correct(i):
        src, dst = chain[i]
        single(1, src, (), dst, rows_of(rf, i), edges if i == 0 else [(first - 8, 40), (first + C - 32, 40)])

    def begin(i):
        for lo in (first - 8, first + C - 32):
            sa[i, pl.ds(lo, 40), :] = hold[i, pl.ds(lo - first + 8, 40), :] + starts[i][pl.ds(lo, 40), :]
        if i:
            out[4 * i - 1] = sa[i, main, :]

    def relax(i, level):
        for lo, n in ((first - 8, 40), (first + C - 32, 40)) if level < 2 else ((first, 32), (first + C - 32, 32)):
            levels[level + 1][i, pl.ds(lo, n), :] = (
                heun(coef, 0, levels[level], (i,), lo, n) + source(level, i, lo - first, n))
        out[4 * i + level] = levels[level + 1][i, main, :]

    begin(0)
    correct(0)
    relax(0, 0)
    begin(1)
    correct(1)
    relax(0, 1)
    relax(1, 0)
    begin(2)
    correct(2)
    relax(0, 2)
    relax(1, 1)
    relax(2, 0)
    begin(3)
    relax(1, 2)
    relax(2, 1)
    relax(3, 0)
    relax(2, 2)
    relax(3, 1)
    relax(3, 2)
    pl.when(sx == 1)(lambda: arrive(*edge_2))

    @pl.when((sx == 0) | (c == 0))
    def _():
        rl2[...] = jnp.zeros_like(rl2)

    @pl.when((sx == 0) | (c == count - 1))
    def _():
        rr2[...] = jnp.zeros_like(rr2)

    y2f[pl.ds(0, H), :] = yl[pl.ds(H, H), :] + rl2[...]
    y2f[pl.ds(C - H, H), :] = yl[pl.ds(C, H), :] + rr2[...]
    right_after = jnp.where(sx == 0, y1f[main, :], y2f[...])
    own = jnp.concatenate([heun(coef, 2, bf, (), lo, n) for lo, n in inner], 0)
    out[15] = g3[...] + (right_after + jnp.where(place == 1, 0.0, own))

    for up, down in sent:
        told = sx == 1 if up is edge_2[0] else True
        pl.when(told & has_right)(up.wait_send)
        pl.when(told & has_left)(down.wait_send)
    for up, down, told in halo_k + [copies + (sx == 0,) for copies in edge_1]:
        pl.when(told & has_right)(up.wait_send)
        pl.when(told & has_left)(down.wait_send)

    @pl.when(place < 3)
    def _():
        prev_copy.wait_send()

    @pl.when(sx == 0)
    def _():
        hand_in.wait_send()
        for copy in hand_out:
            copy.wait_send()

    @pl.when(place == 1)
    def _():
        for copy in cross_out[0] + cross_out[1]:
            copy.wait_send()
        for up, down in cross_sides:
            pl.when(has_right)(up.wait_send)
            pl.when(has_left)(down.wait_send)

    pl.when(place == 3)(relay.wait_send)


def local(u_init, guess, forcing, speed_x, speed_y, diffusion):
    def vmem(*shape):
        return pltpu.VMEM(shape, F32)

    any_space = pl.BlockSpec(memory_space=pltpu.HBM)
    field = (N, C)
    by_column = pl.pallas_call(
        kernel,
        out_shape=pltpu.VMEM(forcing.shape, F32),
        in_specs=[any_space] * 6,
        out_specs=pl.BlockSpec(memory_space=pltpu.VMEM),
        scratch_shapes=[
            vmem(3, C, C), vmem(C, C), vmem(4, C, C), vmem(16, C, C), vmem(C, C),
            vmem(3, W, C), vmem(5, *field), vmem(3, 13, W, C),
            vmem(12, C + 16, C), vmem(C, C), vmem(4, C, C), vmem(4, C, C),
            *(vmem(4, *field) for _ in range(5)), vmem(3, *field),
            vmem(*field), vmem(*field), vmem(*field),
            vmem(*field), vmem(W, C), vmem(*field), vmem(*field), vmem(C, C),
            vmem(*field), vmem(*field), vmem(*field),
            vmem(2, 2 * H, C), vmem(C - 32, C), vmem(40, C), vmem(40, C), vmem(2 * H, C), vmem(2 * H, C),
            vmem(2 * H, C), vmem(2 * H, C), vmem(H, C), vmem(H, C), vmem(W, C),
            vmem(3, 24, C), vmem(3, 24, C), *(vmem(6, 8, C) for _ in range(4)),
            pltpu.SemaphoreType.DMA((6,)),
            pltpu.SemaphoreType.DMA((28,)),
            pltpu.SemaphoreType.DMA((28,)),
            pltpu.SemaphoreType.DMA((4,)),
            pltpu.SemaphoreType.DMA((4,)),
        ],
        compiler_params=pltpu.CompilerParams(collective_id=0, has_side_effects=True, vmem_limit_bytes=60 << 20),
    )(u_init, guess, forcing, speed_x, speed_y, diffusion)
    return jnp.swapaxes(by_column, 1, 2)


def solution(mesh):
    placed = (
        P(None, "sy"),
        P(("tm", "sx"), None, "sy"),
        P(("tm", "sx"), None, "sy"),
        P(None, "sy"),
        P(None, "sy"),
        P(None, "sy"),
    )
    return jax.shard_map(
        local, mesh=mesh, in_specs=placed, out_specs=P(("tm", "sx"), None, "sy"), check_vma=False
    )
```
